128 devices in a mesh: pipe: 2 (over core), dp: 16 (over y, z), mp: 4 (over x).
Axes of the slice: x: 4, y: 4, z: 4, core: 2. Of those that a mesh axis runs over, the one named last changes fastest.
Arguments:
- states: bfloat16 [2, 32, 512, 512], P('pipe', 'dp', 'mp'), may hold values from -6 to 6
- cotangent: bfloat16 [2, 32, 512, 512], P('pipe', 'dp', 'mp'), may hold values from -6 to 6
- halting: int32 [2, 32, 512], P('pipe', 'dp', 'mp'), may hold values from 0 to 1, as said below
- segments: int32 [2, 32, 512], P(None, 'dp'), may hold values from 0 to 4, as said below
- norm_gain: float32 [2, 3, 512], P('pipe'), may hold values from 0.5 to 1.5
- norm_bias: float32 [2, 3, 512], P('pipe'), may hold values from -1 to 1
- attn_in: bfloat16 [2, 512, 3, 512], P('pipe', 'dp', None, 'mp'), may hold values from -0.25 to 0.25
- attn_out: bfloat16 [2, 512, 512], P('pipe', 'mp', 'dp'), may hold values from -2 to 2
- cross: bfloat16 [2, 512, 2, 512], P('pipe', 'dp', None, 'mp'), may hold values from -6 to 6, as said below
- up_weight: bfloat16 [2, 512, 2048], P('pipe', 'dp', 'mp'), may hold values from -0.25 to 0.25
- up_bias: float32 [2, 2048], P('pipe'), may hold values from -1 to 1
- down_weight: bfloat16 [2, 2048, 512], P('pipe', 'mp', 'dp'), may hold values from -0.125 to 0.125
- down_bias: float32 [2, 512], P('pipe'), may hold values from -1 to 1
- halt_weight: float32 [2, 512], P('pipe'), may hold values from -0.25 to 0.25
- halt_bias: float32 [2], P('pipe'), may hold values from -1 to 1
Outputs:
- states_out: bfloat16 [2, 32, 512, 512], P('pipe', 'dp', 'mp')
- states_grad: float32 [2, 32, 512, 512], P('pipe', 'dp', 'mp')
- norm_gain_grad: float32 [2, 3, 512], P('pipe')
- norm_bias_grad: float32 [2, 3, 512], P('pipe')
- attn_in_grad: float32 [2, 512, 3, 512], P('pipe', 'dp', None, 'mp')
- attn_out_grad: float32 [2, 512, 512], P('pipe', 'mp', 'dp')
- cross_grad: float32 [2, 512, 2, 512], P('pipe', 'dp', None, 'mp')
- up_weight_grad: float32 [2, 512, 2048], P('pipe', 'dp', 'mp')
- up_bias_grad: float32 [2, 2048], P('pipe')
- down_weight_grad: float32 [2, 2048, 512], P('pipe', 'mp', 'dp')
- down_bias_grad: float32 [2, 512], P('pipe')
- halt_weight_grad: float32 [2, 512], P('pipe')
- halt_bias_grad: float32 [2], P('pipe')
- act_stats: float32 [2, 2], P('pipe')
The draws below stay inside these ranges and needn't reach their ends.
Inputs may be any that keep to these rules, and one draw needn't show every extreme that they name: `halting`: a row's first position is always 1. `segments`: document numbers never fall along a row; each row of either side holds all 5 documents, so a target document always has a source document of the same number in the same row; document 2 starts within the first 128 positions of its row and ends within the last 128. `cross`: independent entries of zero mean.
All inputs are finite; a program needn't handle non-finite values.
Results may differ from the reference program's by a relative error of at most 0.023.
Values may be sent and summed in bfloat16 or wider, within the bound.
A program may use at most 128 MiB of HBM per device.

```python
import jax
import jax.numpy as jnp
from jax import lax

D = 512
HEADS = 8
HEAD_DIM = 64
FF = 2048
TOK_DEV = 128
CUTS = 2
LEN = 512
ROWS = 32


def draw_halting(key, part):
    key = jax.random.fold_in(key, 11)
    row_ids = jnp.arange(ROWS, dtype=jnp.int32)[:, None]
    columns = jnp.arange(LEN, dtype=jnp.int32)[None, :]
    level = 250 + 600 * (row_ids * LEN + columns) // (ROWS * LEN)
    draws = jax.random.randint(key, (2, ROWS, LEN), 0, 1000, dtype=jnp.int32)
    runs = (draws < level[None]).astype(jnp.int32)
    return jnp.where(columns[None] == 0, 1, runs).astype(jnp.int32)


def draw_segments(key, part):
    key = jax.random.fold_in(key, 5)
    low_key, high_key = jax.random.split(key)
    span = TOK_DEV - 1

    def cut_points(sub, offset):
        scores = jax.random.randint(sub, (2, ROWS, span), 0, 1 << 20, dtype=jnp.int32) * span
        scores = scores + jnp.arange(span, dtype=jnp.int32)
        _, picks = lax.top_k(scores, CUTS)
        return picks.astype(jnp.int32) + offset
    cuts = jnp.concatenate([cut_points(low_key, 1), cut_points(high_key, LEN - TOK_DEV + 1)], axis=-1)
    columns = jnp.arange(LEN, dtype=jnp.int32)
    return jnp.sum((cuts[..., None] <= columns).astype(jnp.int32), axis=-2).astype(jnp.int32)


def draw_cross(key, part):
    key = jax.random.fold_in(key, 7)
    values = jnp.clip(jax.random.normal(key, (2, D, 2, D), jnp.float32), -6.0, 6.0)
    section_ids = jnp.arange(2)[:, None, None, None]
    slot_ids = jnp.arange(2)[None, None, :, None]
    chosen = jnp.logical_and(section_ids == 1, slot_ids == 1)
    scale = jnp.where(chosen, max(D // 64, 1) ** (-0.5), D ** (-0.5))
    return (values * scale).astype(jnp.bfloat16)


def levels(own_key, shape, pieces, least, high):
    loudness, own = 1.0, jax.random.fold_in(own_key, 6)
    for axis_at, blocks in pieces:
        steps = jnp.exp(jax.random.uniform(jax.random.fold_in(own, axis_at), (blocks,), jnp.float32, least / len(pieces), high / len(pieces)))
        loudness = loudness * jnp.repeat(steps, shape[axis_at] // blocks).reshape([-1 if axis == axis_at else 1 for axis in range(len(shape))])
    return loudness


def scatter_about(key, shape, scale, limit, shards=(), kind=jnp.bfloat16):
    level = levels(key, shape, shards, -0.22, 0.18) if shards else 1.0
    values = jax.random.normal(key, shape, jnp.float32) * scale * level
    return jnp.minimum(jnp.maximum(values, -limit), limit).astype(kind)


def setup_inputs(seed: int = 0) -> dict:
    arg_keys = jax.random.split(jax.random.key(seed), 16)
    states = scatter_about(arg_keys[0], (2, ROWS, LEN, D), 1.0, 6.0, ((0, 2), (1, 16), (2, 4)))
    cotangent = scatter_about(arg_keys[1], (2, ROWS, LEN, D), 1.0, 6.0, ((0, 2), (1, 16), (2, 4)))
    halting = draw_halting(jax.random.fold_in(arg_keys[15], 71), 0)
    segments = draw_segments(jax.random.fold_in(arg_keys[15], 71), 0)
    norm_gain = jnp.clip(1.0 + 0.1 * jax.random.normal(arg_keys[4], (2, 3, D), jnp.float32), 0.5, 1.5)
    norm_bias = scatter_about(arg_keys[5], (2, 3, D), 0.2, 1.0, ((0, 2),), jnp.float32)
    attn_in = scatter_about(arg_keys[6], (2, D, 3, D), D ** -0.5, 0.25, ((0, 2), (1, 16), (3, 4)))
    attn_out = scatter_about(arg_keys[7], (2, D, D), (max(D // 64, 1)) ** -0.5, 2.0, ((0, 2), (1, 4), (2, 16)))
    cross = draw_cross(jax.random.fold_in(arg_keys[15], 71), 0)
    up_weight = scatter_about(arg_keys[9], (2, D, FF), D ** -0.5, 0.25, ((0, 2), (1, 16), (2, 4)))
    up_bias = scatter_about(arg_keys[10], (2, FF), 0.2, 1.0, ((0, 2),), jnp.float32)
    down_weight = scatter_about(arg_keys[11], (2, FF, D), FF ** -0.5, 0.125, ((0, 2), (1, 4), (2, 16)))
    down_bias = scatter_about(arg_keys[12], (2, D), 0.2, 1.0, ((0, 2),), jnp.float32)
    halt_weight = scatter_about(arg_keys[13], (2, D), D ** -0.5, 0.25, ((0, 2),), jnp.float32)
    halt_bias = jnp.clip(jax.random.uniform(arg_keys[14], (2,), jnp.float32, -1.0, 1.0) * levels(arg_keys[14], (2,), ((0, 2),), -0.4, 0.0), -1.0, 1.0)
    return dict(states=states, cotangent=cotangent, halting=halting, segments=segments, norm_gain=norm_gain, norm_bias=norm_bias, attn_in=attn_in, attn_out=attn_out, cross=cross, up_weight=up_weight, up_bias=up_bias, down_weight=down_weight, down_bias=down_bias, halt_weight=halt_weight, halt_bias=halt_bias)


EPS = 1e-06

@jax.custom_vjp
def low(v):
    return lax.optimization_barrier(v.astype(jnp.bfloat16)).astype(jnp.float32)

@jax.custom_vjp
def low_back(v):
    return v

def low_keep(v):
    return (low(v), None)

def low_pass(kept, grad):
    return (grad,)

def back_keep(v):
    return (v, None)

def back_low(kept, grad):
    return (low(grad),)
low.defvjp(low_keep, low_pass)
low_back.defvjp(back_keep, back_low)

def matmul(left, right):
    return jnp.dot(left, right, precision=lax.Precision.HIGHEST, preferred_element_type=jnp.float32)

def layer_norm(value, gain, shift):
    center = value - lax.optimization_barrier(jnp.mean(value, axis=-1, keepdims=True))
    spread = lax.optimization_barrier(jnp.mean(center * center, axis=-1, keepdims=True))
    return center * lax.rsqrt(spread + EPS) * gain + shift

def attend(queries, key_rows, values, allowed):
    scores = low_back(jnp.einsum('qhd,khd->hqk', queries, key_rows, precision=lax.Precision.HIGHEST, preferred_element_type=jnp.float32)) * HEAD_DIM ** (-0.5)
    scores = jnp.where(allowed[None], scores, -1e+30)
    probs = jax.nn.softmax(scores, axis=-1)
    return jnp.einsum('hqk,khd->qhd', low(probs), values, precision=lax.Precision.HIGHEST, preferred_element_type=jnp.float32)

def self_block(params, section, inputs, seg_row, causal):
    gains, shifts, w_in, w_out = (params[0], params[1], params[2], params[3])
    normed = low(layer_norm(inputs, gains[section, 0], shifts[section, 0]))
    proj = low_back(low(matmul(normed, w_in[section].reshape(D, 3 * D)))).reshape(LEN, 3, HEADS, HEAD_DIM)
    allowed = seg_row[:, None] == seg_row[None, :]
    if causal:
        allowed = jnp.logical_and(allowed, jnp.arange(LEN)[:, None] >= jnp.arange(LEN)[None, :])
    heads = low_back(low(attend(proj[:, 0], proj[:, 1], proj[:, 2], allowed))).reshape(LEN, D)
    return inputs + low_back(matmul(heads, w_out[section]))

def ffn_block(params, section, inputs):
    gains, shifts = (params[0], params[1])
    w_up, b_up, w_down, b_down = (params[5], params[6], params[7], params[8])
    normed = low(layer_norm(inputs, gains[section, 2], shifts[section, 2]))
    pre = low_back(matmul(normed, w_up[section])) + b_up[section]
    act = low(jax.nn.gelu(pre))
    return inputs + low_back(matmul(act, w_down[section])) + b_down[section]

def halt_step(params, section, inputs, result, running):
    h_w, h_b = (params[9], params[10])
    prob = jax.nn.sigmoid(jnp.dot(inputs, h_w[section], precision=lax.Precision.HIGHEST) + h_b[section])
    return (inputs + (running * prob)[:, None] * (result - inputs), jnp.sum(running * prob))

def row_fn(params, source, target, run_src, run_tgt, seg_src, seg_tgt):
    gains, shifts, w_cross = (params[0], params[1], params[4])
    enc = ffn_block(params, 0, self_block(params, 0, source, seg_src, False))
    enc_out, enc_sum = halt_step(params, 0, source, enc, run_src)
    memory = layer_norm(enc_out, gains[0, 1], shifts[0, 1])
    pairs = low_back(low(matmul(low(memory), w_cross[0].reshape(D, 2 * D)))).reshape(LEN, 2, HEADS, HEAD_DIM)
    after_self = self_block(params, 1, target, seg_tgt, True)
    normed = low(layer_norm(after_self, gains[1, 1], shifts[1, 1]))
    queries = low_back(low(matmul(normed, w_cross[1][:, 0]))).reshape(LEN, HEADS, HEAD_DIM)
    allowed = seg_tgt[:, None] == seg_src[None, :]
    heads = low_back(low(attend(queries, pairs[:, 0], pairs[:, 1], allowed))).reshape(LEN, D)
    after_cross = after_self + low_back(matmul(heads, w_cross[1][:, 1].T))
    dec = ffn_block(params, 1, after_cross)
    dec_out, dec_sum = halt_step(params, 1, target, dec, run_tgt)
    return ((memory, dec_out), (enc_sum, jnp.sum(run_src), dec_sum, jnp.sum(run_tgt)))

def reference(states, cotangent, halting, segments, norm_gain, norm_bias, attn_in, attn_out, cross, up_weight, up_bias, down_weight, down_bias, halt_weight, halt_bias):
    params = tuple((arr.astype(jnp.float32) for arr in (norm_gain, norm_bias, attn_in, attn_out, cross, up_weight, up_bias, down_weight, down_bias, halt_weight, halt_bias)))
    source = states[0].astype(jnp.float32)
    target = states[1].astype(jnp.float32)
    running = halting.astype(jnp.float32)

    def whole(weights, src_all, tgt_all):

        def step(carry, entry):
            return (carry, jax.checkpoint(row_fn)(weights, *entry))
        _, (outs, sums) = lax.scan(step, None, (src_all, tgt_all, running[0], running[1], segments[0], segments[1]))
        return (outs, sums)
    (memory, stepped), pull, sums = jax.vjp(whole, params, source, target, has_aux=True)
    grads, d_source, d_target = pull((cotangent[0].astype(jnp.float32), cotangent[1].astype(jnp.float32)))
    stats = []
    for section in range(2):
        total_run = jnp.sum(sums[2 * section])
        total_count = jnp.sum(sums[2 * section + 1])
        stats.append(jnp.stack([total_run / total_count, 1.0 - total_count / (ROWS * LEN)]))
    return (jnp.stack([memory, stepped]).astype(jnp.bfloat16), jnp.stack([d_source, d_target]), grads[0], grads[1], grads[2], grads[3], grads[4], grads[5], grads[6], grads[7], grads[8], grads[9], grads[10], jnp.stack(stats))
```

```python
import jax
import jax.numpy as jnp
from jax import lax
from jax.experimental import pallas as pl
from jax.experimental.pallas import tpu as pltpu
from jax.sharding import PartitionSpec as P

MESH = pl.DeviceIdType.MESH
BF = jnp.bfloat16
F32 = jnp.float32
EPS = 1e-06
T = 512
SCALE = 0.125
WIDTHS = (512, 1024, 512)

GAIN, SHIFT, UPB, DOWNB, HALTW, SCAL = 0, 3, 6, 10, 11, 12
SMALL = 16

SCRATCH = dict(
    PSB=((32, 512), BF),
    PFB=((32, 1024), BF),
    PCB=((32, 256), BF),
    PK=((SMALL, T), F32),
    HB=((2, 16, 128), BF),
    HL=((4, 16, 128), BF),
    RN=((T, 128), F32),
    IN=((T, T), BF),
    COT=((T, T), BF),
    PSIB=((SMALL, T), F32),
    PV=((SMALL, T), F32),
    W0=((2, 4, 4, 32, 512), BF),
    W1=((2, 4, 4, 32, 1024), BF),
    W2=((2, 4, 4, 32, 512), BF),
    U=((3, T, T), F32),
    F=((3, T, 128), F32),
    N=((3, T, T), BF),
    NT=((3, T, T), BF),
    QKV=((2, T, 384), BF),
    KT=((2, 128, T), BF),
    VT=((2, 128, T), BF),
    HD=((2, T, 128), BF),
    PA=((2, 2, T, T), BF),
    CQ=((2, T, 128), BF),
    CKV=((2, T, 256), BF),
    CKT=((2, 128, T), BF),
    CVT=((2, 128, T), BF),
    HX=((2, T, 128), BF),
    PX=((2, 2, T, T), BF),
    AS=((T, T), F32),
    DIF=((T, T), F32),
    GP=((2, T, T), F32),
    ACT=((2, T, T), BF),
    PB=((2, T, T), BF),
    DA=((T, T), F32),
    DX=((T, T), F32),
    FF=((T, T), BF),
    FB=((T, T), BF),
    LT=((T, T), BF),
    XS=((3, T, T), BF),
    XR=((3, T, T), BF),
    BS=((T, T), F32),
    BX=((T, T), F32),
    MEM=((T, T), BF),
    MT=((T, T), BF),
    DM=((T, T), BF),
    DS=((T, T), BF),
    DSR=((T, T), BF),
    DSO=((T, T), BF),
    DQ=((2, T, 384), BF),
    DH=((2, T, 128), BF),
    DSB=((2, T, T), BF),
    PR=((T, 128), F32),
    OB=((T, T), BF),
    DXB=((T, T), BF),
    G0=((2, 4, 4, 32, 512), BF),
    G1=((2, 4, 4, 32, 1024), BF),
    G2=((2, 4, 4, 32, 512), BF),
    LA0=((2, 3, 4, 32, 512), BF),
    LA1=((2, 3, 4, 32, 1024), BF),
    LA2=((2, 3, 4, 32, 512), BF),
    SA0=((2, 4, 32, 512), BF),
    SA1=((2, 4, 32, 1024), BF),
    SA2=((2, 4, 32, 512), BF),
    LB0=((2, 3, 32, 512), BF),
    LB1=((2, 3, 32, 1024), BF),
    LB2=((2, 3, 32, 512), BF),
    SB0=((2, 32, 512), BF),
    SB1=((2, 32, 1024), BF),
    SB2=((2, 32, 512), BF),
    SM=((SMALL, T), F32),
    LM1=((3, SMALL, T), F32),
    SM2=((SMALL, T), F32),
    LM2=((3, SMALL, T), F32),
    SM3=((SMALL, T), F32),
)

SEMS = dict(
    pp=(1,),
    g0=(2, 4),
    pf=(2,),
    pc=(2, 2),
    po=(2,),
    rk=(2, 2),
    st=(4,),
    hl=(4,),
    ct=(4,),
    lo=(6,),
    ga=(3, 2, 2, 3),
    ex=(3, 4),
    mem=(4, 2),
    mfw=(4,),
    dmx=(4,),
    dme=(4, 2),
    dmf=(4,),
    rs=(3, 2, 2, 3),
    rc=(3, 2),
    os=(2,),
    od=(2,),
    m1=(3,),
    m2=(3,),
    m3=(4,),
)


def mm(a, b):
    return lax.dot_general(a, b, (((1,), (0,)), ((), ())), preferred_element_type=F32)


def mm_nt(a, b):
    return lax.dot_general(a, b, (((1,), (1,)), ((), ())), preferred_element_type=F32)


def mm_tn(a, b):
    return lax.dot_general(a, b, (((0,), (0,)), ((), ())), preferred_element_type=F32)


def rows_of(i, size):
    return pl.ds(pl.multiple_of(i * size, size), size)


def loop(count, body):
    lax.fori_loop(0, count, lambda i, _: (body(i), 0)[1], 0)


def wide(v):
    return jnp.concatenate([v, v, v, v], axis=1)


def mean(v):
    return jnp.mean(v, axis=-1, keepdims=True)


class Refs:
    pass


def kernel(*refs):
    (states, cot, halts, seg, gain, shift, upb, downb, haltw, haltb, w_in, w_out, w_cross, w_up, w_down,
     o_st, o_dx, o_c0, o_c1, o_c2, o_sm) = refs[:21]
    r = Refs()
    rest = refs[21:]
    for name, ref in zip(SCRATCH, rest):
        setattr(r, name, ref)
    rest = rest[len(SCRATCH):]
    ss, rs = {}, {}
    for k, name in enumerate(SEMS):
        ss[name], rs[name] = rest[2 * k], rest[2 * k + 1]
    W, G = (r.W0, r.W1, r.W2), (r.G0, r.G1, r.G2)
    LA, SA = (r.LA0, r.LA1, r.LA2), (r.SA0, r.SA1, r.SA2)
    LB, SB = (r.LB0, r.LB1, r.LB2), (r.SB0, r.SB1, r.SB2)
    LC = (o_c0, o_c1, o_c2)

    c = lax.axis_index("pipe")
    dp = lax.axis_index("dp")
    x = lax.axis_index("mp")
    y, z = dp // 4, lax.rem(dp, 4)
    dec = jnp.logical_or(x == 1, x == 2)
    enc = jnp.logical_not(dec)
    role = jnp.where(dec, 1, 0)
    m = x // 2
    sib = 1 - c
    pair = x + 1 - 2 * lax.rem(x, 2)
    zs = [lax.rem(z + d, 4) for d in range(4)]
    zb = [lax.rem(z + 4 - d, 4) for d in range(4)]
    ys = [lax.rem(y + d, 4) for d in range(4)]
    yb = [lax.rem(y + 4 - d, 4) for d in range(4)]

    def dev(core=c, yy=y, zz=z, xx=x):
        return (core, yy * 4 + zz, xx)

    def rdma(src, dst, ssem, rsem, to):
        return pltpu.make_async_remote_copy(
            src_ref=src, dst_ref=dst, send_sem=ssem, recv_sem=rsem, device_id=to, device_id_type=MESH
        )

    ends = []

    def put(what, when=None):
        rdma(*what()).start()

        def end():
            if when is None:
                rdma(*what()).wait_send()
            else:
                @pl.when(when)
                def _():
                    rdma(*what()).wait_send()

        ends.append(end)

    def put_or_keep(what, when=None):
        def away():
            core, xx = what()[4:]
            return jnp.logical_not(jnp.logical_and(core == c, xx == x))

        @pl.when(jnp.logical_not(away()))
        def _():
            src, dst, _, rsem, _, _ = what()
            pltpu.make_async_copy(src, dst, rsem).start()

        def remote():
            src, dst, ssem, rsem, core, xx = what()
            return rdma(src, dst, ssem, rsem, dev(core, xx=xx))

        @pl.when(away())
        def _():
            remote().start()

        def end():
            out = away()
            if when is not None:
                out = jnp.logical_and(out, when)

            @pl.when(out)
            def _():
                remote().wait_send()

        ends.append(end)

    def got(dst, rsem):
        pltpu.make_async_copy(dst, dst, rsem).wait()

    barrier = pltpu.get_barrier_semaphore()
    partners = [dev(zz=zs[d]) for d in (1, 2, 3)] + [dev(yy=ys[d]) for d in (1, 2, 3)]
    partners += [dev(core=sib, xx=lax.rem(x + d, 4)) for d in range(4)]
    partners += [dev(xx=lax.rem(x + d, 4)) for d in (1, 2, 3)]
    jj_me = lax.rem(x, 2)
    to_y = [jnp.where(jj_me == 0, y, ys[d]) for d in range(4)]
    to_z = [jnp.where(jj_me == 0, zs[d], z) for d in range(4)]
    for d in (1, 2, 3):
        partners.append(dev(core=role, zz=zb[d], xx=2 * c))
        partners.append(dev(core=role, yy=yb[d], xx=2 * c + 1))
    for to in partners:
        pl.semaphore_signal(barrier, inc=1, device_id=to, device_id_type=MESH)

    staged = [
        (w_in.at[0], r.PSB.at[:, pl.ds(0, 128)]), (w_in.at[1], r.PSB.at[:, pl.ds(128, 128)]),
        (w_in.at[2], r.PSB.at[:, pl.ds(256, 128)]), (w_out, r.PSB.at[:, pl.ds(384, 128)]),
        (w_up, r.PFB.at[:, pl.ds(0, 512)]), (w_down, r.PFB.at[:, pl.ds(512, 512)])]
    staged = [pltpu.make_async_copy(a, b, rs["lo"].at[k]) for k, (a, b) in enumerate(staged)]
    for copy in staged:
        copy.start()
    r.PK[GAIN:GAIN + 3] = gain[:, 0, :]
    r.PK[SHIFT:SHIFT + 3] = shift[:, 0, :]
    r.PK[UPB:UPB + 4] = upb[:, 0, :]
    r.PK[DOWNB:DOWNB + 1] = downb[...]
    r.PK[HALTW:HALTW + 1] = haltw[...]
    r.PK[SCAL:SCAL + 1] = jnp.broadcast_to(haltb[...], (1, T))
    r.PK[SCAL + 1:SMALL] = jnp.zeros((SMALL - SCAL - 1, T), F32)
    for k in (0, 1):
        r.HB[k] = jnp.broadcast_to(halts[k:k + 1].astype(F32), (16, 128)).astype(BF)
    crossed = w_cross[...].astype(F32)
    for k in (0, 1):
        r.PCB[:, 128 * k:128 * k + 128] = crossed[:, k, :].astype(BF)
    for copy in staged:
        copy.wait()
    pl.semaphore_wait(barrier, len(partners))

    homes = (c, 3 - c)

    def gather_first(g):
        for d in (1, 2, 3):
            put(lambda d=d: (W[g].at[0, y, z], W[g].at[0, y, z], ss["ga"].at[g, 0, 0, d - 1], rs["ga"].at[g, 0, 0, d - 1], dev(zz=zs[d])), dec if g == 2 else None)
            put(lambda d=d: (W[g].at[1, y, z], W[g].at[1, y, z], ss["ga"].at[g, 0, 1, d - 1], rs["ga"].at[g, 0, 1, d - 1], dev(yy=ys[d])), dec if g == 2 else None)

    def gather_second(g):
        for d in range(4):
            if g == 0:
                got(W[g].at[0, y, zb[d]], rs["g0"].at[0, d])
                got(W[g].at[1, yb[d], z], rs["g0"].at[1, d])
            elif d > 0:
                got(W[g].at[0, y, zb[d]], rs["ga"].at[g, 0, 0, d - 1])
                got(W[g].at[1, yb[d], z], rs["ga"].at[g, 0, 1, d - 1])
        for d in (1, 2, 3):
            put(lambda d=d: (W[g].at[0, y], W[g].at[0, y], ss["ga"].at[g, 1, 0, d - 1], rs["ga"].at[g, 1, 0, d - 1], dev(yy=ys[d])), dec if g == 2 else None)
            put(lambda d=d: (W[g].at[1, :, z], W[g].at[1, :, z], ss["ga"].at[g, 1, 1, d - 1], rs["ga"].at[g, 1, 1, d - 1], dev(zz=zs[d])), dec if g == 2 else None)

    def gather_done(g):
        for d in (1, 2, 3):
            got(W[g].at[0, yb[d]], rs["ga"].at[g, 1, 0, d - 1])
            got(W[g].at[1, :, zb[d]], rs["ga"].at[g, 1, 1, d - 1])

    def reduce_first(g, jj, when=None):
        for d in (1, 2, 3):
            def what(d=d):
                src, to = (G[g].at[0, ys[d]], dev(yy=ys[d])) if jj == 0 else (G[g].at[1, :, zs[d]], dev(zz=zs[d]))
                return src, LA[g].at[jj, d - 1], ss["rs"].at[g, 0, jj, d - 1], rs["rs"].at[g, 0, jj, d - 1], to

            put(what, when)

    def reduce_second(g):
        for jj in (0, 1):
            for d in (1, 2, 3):
                got(LA[g].at[jj, d - 1], rs["rs"].at[g, 0, jj, d - 1])

            def add(k):
                own = G[g][0, y, k] if jj == 0 else G[g][1, k, z]
                total = own.astype(F32)
                for d in range(3):
                    total = total + LA[g][jj, d, k].astype(F32)
                SA[g][jj, k] = total.astype(BF)

            loop(4, add)
            for d in (1, 2, 3):
                def what(d=d, jj=jj):
                    src, to = (SA[g].at[0, zs[d]], dev(zz=zs[d])) if jj == 0 else (SA[g].at[1, ys[d]], dev(yy=ys[d]))
                    return src, LB[g].at[jj, d - 1], ss["rs"].at[g, 1, jj, d - 1], rs["rs"].at[g, 1, jj, d - 1], to

                put(what, dec if g == 2 else None)

    def reduce_third(g):
        for jj in (0, 1):
            for d in (1, 2, 3):
                got(LB[g].at[jj, d - 1], rs["rs"].at[g, 1, jj, d - 1])
            total = (SA[g][0, z] if jj == 0 else SA[g][1, y]).astype(F32)
            for d in range(3):
                total = total + LB[g][jj, d].astype(F32)
            SB[g][jj] = total.astype(BF)
            if g == 2:
                for k in (0, 1):
                    put_or_keep(lambda jj=jj, k=k: (
                        SB[g].at[jj, :, pl.ds(256 * k, 256)], LC[g].at[m], ss["rk"].at[k, jj], rs["rc"].at[g, m],
                        k, 2 * c + jj), dec)
            else:
                put_or_keep(lambda jj=jj: (
                    SB[g].at[jj], LC[g].at[m], ss["rc"].at[g, jj], rs["rc"].at[g, m], role, 2 * c + jj))

    def half_rows(i, core):
        return pl.ds(pl.multiple_of(128 * i + 64 * core, 64), 64)

    def memory_copy(i):
        part = half_rows(i, c)
        return rdma(r.N.at[1, part], r.MEM.at[part], ss["mem"].at[i, 0], rs["mem"].at[i, c], dev(xx=pair))

    def memory_forward(i):
        part = half_rows(i, c)
        return rdma(r.MEM.at[part], r.MEM.at[part], ss["mfw"].at[i], rs["mem"].at[i, c], dev(core=sib))

    def memory_grad_swap(i):
        part = half_rows(i, sib)
        return rdma(r.DS.at[part], r.DSR.at[part], ss["dmx"].at[i], rs["dmx"].at[i], dev(core=sib))

    def memory_grad_copy(i):
        part = half_rows(i, c)
        return rdma(r.DSO.at[part], r.DM.at[part], ss["dme"].at[i, 0], rs["dme"].at[i, c], dev(xx=pair))

    def memory_grad_forward(i):
        part = half_rows(i, c)
        return rdma(r.DM.at[part], r.DM.at[part], ss["dmf"].at[i], rs["dme"].at[i, c], dev(core=sib))

    def exchange_copy(k, i):
        part = rows_of(i, 128)
        return rdma(r.XS.at[k, part], r.XR.at[k, part], ss["ex"].at[k, i], rs["ex"].at[k, i], dev(core=sib))

    for d in range(4):
        for k in (0, 1):
            if d == 0:
                put_or_keep(lambda k=k: (
                    r.PSB, r.W0.at[jj_me, y, z], ss["g0"].at[k, 0], rs["g0"].at[jj_me, 0], x // 2, homes[k]))
            else:
                put(lambda k=k, d=d: (
                    r.PSB, r.W0.at[jj_me, y, z], ss["g0"].at[k, d], rs["g0"].at[jj_me, d],
                    dev(core=x // 2, yy=to_y[d], zz=to_z[d], xx=homes[k])))
    for k in (0, 1):
        put_or_keep(lambda k=k: (
            r.PFB, r.W1.at[jj_me, y, z], ss["pf"].at[k], rs["pf"].at[jj_me], x // 2, homes[k]))
    put(lambda: (r.PK, r.PSIB, ss["pp"].at[0], rs["pp"].at[0], dev(core=sib)))
    r.SM[...] = jnp.zeros((SMALL, T), F32)
    for jj in (0, 1):
        got(r.W1.at[jj, y, z], rs["pf"].at[jj])
    gather_first(1)
    for k in (0, 1):
        for core in (0, 1):
            put_or_keep(lambda k=k, core=core: (
                states.at[k], r.IN.at[rows_of(x, 128)], ss["st"].at[2 * k + core], rs["st"].at[x], core, homes[k]))
            put_or_keep(lambda k=k, core=core: (
                r.HB.at[k], r.HL.at[x], ss["hl"].at[2 * k + core], rs["hl"].at[x], core, homes[k]))
    gather_second(0)
    for k in (0, 1):
        put_or_keep(lambda k=k: (
            r.PCB, r.W2.at[jj_me, y, z, :, pl.ds(pl.multiple_of(256 * c, 256), 256)], ss["po"].at[k],
            rs["pc"].at[jj_me, c], x // 2, k + 1))
    gather_second(1)
    for k in (0, 1):
        for core in (0, 1):
            put_or_keep(lambda k=k, core=core: (
                cot.at[k], r.COT.at[rows_of(x, 128)], ss["ct"].at[2 * k + core], rs["ct"].at[x], core, homes[k]))
    got(r.PSIB, rs["pp"].at[0])
    r.PV[...] = jnp.where(c == role, r.PK[...], r.PSIB[...])
    for q in range(4):
        got(r.IN.at[pl.ds(128 * q, 128)], rs["st"].at[q])
        got(r.HL.at[q], rs["hl"].at[q])

    def param(row):
        return r.PV[pl.ds(row, 1), :]

    def ln_to(li, part, size, v):
        center = v - mean(v)
        factor = lax.rsqrt(mean(center * center) + EPS)
        unit = center * factor
        normed = unit * param(GAIN + li) + param(SHIFT + li)
        r.U[li, part] = unit
        r.F[li, part] = jnp.broadcast_to(factor, (size, 128))
        r.N[li, part] = normed.astype(BF)

    def count(row, v):
        r.SM[pl.ds(row, 1), :] += jnp.sum(v, axis=0, keepdims=True)

    def ln_back(li, part, n):
        unit, factor = r.U[li, part], wide(r.F[li, part])
        scaled = n * param(GAIN + li)
        count(GAIN + li, n * unit)
        count(SHIFT + li, n)
        return factor * (scaled - mean(scaled) - unit * mean(scaled * unit))

    def weight(g, jj, lo, hi):
        return W[g][jj, :, :, :, lo:hi].reshape(T, hi - lo)

    def both(g, lo, hi):
        return jnp.concatenate([weight(g, 0, lo, hi), weight(g, 1, lo, hi)], axis=1)

    def send_part(k, i, size, value):
        r.XS[k, rows_of(i, size)] = value.astype(BF)
        for h in range(size // 128):
            exchange_copy(k, i * (size // 128) + h).start()

    def received(k, part):
        return r.XS[k, part].astype(F32) + r.XR[k, part].astype(F32)

    def after_exchange(k, i, body):
        def one(h):
            exchange_copy(k, 2 * i + h).wait()
            body(rows_of(2 * i + h, 128))

        loop(2, one)

    low_lane = lax.broadcasted_iota(jnp.int32, (1, 128), 1) < 64

    def head_part(v, hh):
        return jnp.where(low_lane if hh == 0 else jnp.logical_not(low_lane), v, jnp.zeros_like(v))

    def attend(q_of, kv, k_at, vt, bias, probs, heads):
        for jj in (0, 1):
            q, keys = q_of(jj), kv[jj, :, k_at:k_at + 128]
            outs = []
            for hh in (0, 1):
                s = mm_nt(keys, head_part(q, hh)) + bias[...]
                e = jnp.exp(s - jnp.max(s, axis=0, keepdims=True))
                w = (e * (1.0 / jnp.sum(e, axis=0, keepdims=True))).astype(BF)
                probs[jj, hh] = w
                outs.append(mm(vt[jj, 64 * hh:64 * hh + 64, :], w))
            heads[jj] = jnp.concatenate(outs, axis=0).T.astype(BF)

    def attend_back(q_of, kv, v_at, kt, probs, dq_at, dk_at, dv_at):
        for jj in (0, 1):
            q, o, values = q_of(jj), r.DH[jj], kv[jj, :, v_at:v_at + 128]
            for hh in (0, 1):
                w = probs[jj, hh].astype(F32)
                wd = w * mm_nt(values, head_part(o, hh))
                delta = jnp.sum(wd, axis=0, keepdims=True)
                r.DSB[hh] = (wd - w * delta).astype(BF)
            dks = [mm(r.DSB[hh], q) for hh in (0, 1)]
            dvs = [mm(probs[jj, hh], o) for hh in (0, 1)]
            dqs = [mm(kt[jj, 64 * hh:64 * hh + 64, :], r.DSB[hh]) for hh in (0, 1)]
            r.DQ[jj, :, dk_at:dk_at + 128] = jnp.where(low_lane, dks[0], dks[1]).astype(BF)
            r.DQ[jj, :, dv_at:dv_at + 128] = jnp.where(low_lane, dvs[0], dvs[1]).astype(BF)
            r.DQ[jj, :, dq_at:dq_at + 128] = (jnp.concatenate(dqs, axis=0).T * SCALE).astype(BF)

    def flip(target, source):
        def one(i):
            part = rows_of(i, 128)
            target[part, :] = source[:, part].T

        loop(4, one)

    def outer(g, jj, lo, hi, left_t, right):
        def one(h):
            total = mm(left_t[rows_of(h, 256), :], right())
            G[g][jj, pl.ds(2 * h, 2), :, :, lo:hi] = total.astype(BF).reshape(2, 4, 32, hi - lo)

        loop(2, one)

    def first(i):
        part = rows_of(i, 128)
        v = r.IN[part].astype(F32)
        ln_to(0, part, 128, v)
        logit = jnp.sum(v * param(HALTW), axis=-1, keepdims=True) + param(SCAL)[:, 0:1]
        r.PR[part] = jnp.broadcast_to(jax.nn.sigmoid(logit), (128, 128))
        r.RN[part] = mm_tn(r.HL[i], jnp.full((16, 128), 1.0 / 16.0, BF))

    loop(4, first)

    docs = lax.broadcasted_iota(jnp.int32, (16, T), 0)
    seg_src, seg_tgt = seg[0, pl.ds(m, 1), :], seg[1, pl.ds(m, 1), :]
    own_src = jnp.where(docs == seg_src, 1.0, 0.0).astype(BF)
    own_tgt = jnp.where(docs == seg_tgt, 1.0, 0.0).astype(BF)
    own_self = jnp.where(enc, own_src, own_tgt)
    k_at = lax.broadcasted_iota(jnp.int32, (T, T), 1)
    q_at = lax.broadcasted_iota(jnp.int32, (T, T), 0)
    reach = jnp.where(enc, T, 0)
    same = jnp.logical_and(mm_tn(own_self, own_self) > 0.5, q_at <= k_at + reach)
    r.BS[...] = jnp.where(same, 0.0, -1e30)

    @pl.when(dec)
    def _():
        r.BX[...] = jnp.where(mm_tn(own_src, own_tgt) > 0.5, 0.0, -1e30)

    @pl.when(dec)
    def _():
        for jj in (0, 1):
            for k in (0, 1):
                got(r.W2.at[jj, y, z, :, pl.ds(256 * k, 256)], rs["pc"].at[jj, k])
        gather_first(2)

    gather_done(0)

    for jj in (0, 1):
        def project(i):
            part = rows_of(i, 256)
            three = mm(r.N[0, part], weight(0, jj, 0, 384))
            r.QKV[jj, part, 0:128] = (three[:, 0:128] * SCALE).astype(BF)
            r.QKV[jj, part, 128:384] = three[:, 128:384].astype(BF)
            r.KT[jj, :, part] = three[:, 128:256].T.astype(BF)
            r.VT[jj, :, part] = three[:, 256:384].T.astype(BF)

        loop(2, project)

    attend(lambda jj: r.QKV[jj, :, 0:128], r.QKV, 128, r.VT, r.BS, r.PA, r.HD)

    @pl.when(dec)
    def _():
        gather_second(2)

    def self_out(i):
        part = rows_of(i, 256)
        heads = jnp.concatenate([r.HD[0, part], r.HD[1, part]], axis=1)
        send_part(0, i, 256, mm_nt(heads, both(0, 384, 512)))

    loop(2, self_out)
    second = jnp.where(enc, 2, 1)

    def self_after(part):
        v = r.IN[part].astype(F32) + received(0, part)
        r.AS[part] = v
        ln_to(second, part, 128, v)

    @pl.when(dec)
    def _():
        gather_done(2)
        loop(2, lambda i: after_exchange(0, i, self_after))
        for jj in (0, 1):
            def ask(i):
                part = rows_of(i, 256)
                r.CQ[jj, part] = (mm(r.N[1, part], weight(2, jj, 256, 384)) * SCALE).astype(BF)

            loop(2, ask)
        flip(r.NT.at[0], r.N.at[0])

        def memory_in(i):
            @pl.when(i < 4)
            def _():
                got(r.MEM.at[half_rows(i, c)], rs["mem"].at[i, c])
                memory_forward(i).start()

            @pl.when(i > 0)
            def _():
                j = i - 1
                got(r.MEM.at[half_rows(j, sib)], rs["mem"].at[j, sib])
                part = rows_of(j, 128)
                for jj in (0, 1):
                    pairs = mm(r.MEM[part], weight(2, jj, 0, 256))
                    r.CKV[jj, part] = pairs.astype(BF)
                    r.CKT[jj, :, part] = pairs[:, 0:128].T.astype(BF)
                    r.CVT[jj, :, part] = pairs[:, 128:256].T.astype(BF)

        loop(5, memory_in)
        attend(lambda jj: r.CQ[jj], r.CKV, 0, r.CVT, r.BX, r.PX, r.HX)

        def cross_out(i):
            part = rows_of(i, 256)
            heads = jnp.concatenate([r.HX[0, part], r.HX[1, part]], axis=1)
            send_part(2, i, 256, mm_nt(heads, both(2, 384, 512)))

        loop(2, cross_out)

    gather_done(1)

    def cross_after(part):
        v = r.AS[part] + received(2, part)
        r.AS[part] = v
        ln_to(2, part, 128, v)

    def ffn(i):
        pl.when(enc)(lambda: after_exchange(0, i, self_after))
        pl.when(dec)(lambda: after_exchange(2, i, cross_after))
        part = rows_of(i, 256)
        total = None
        for jj in (0, 1):
            bias = r.PV[pl.ds(UPB + 2 * c + jj, 1), :]
            u = mm(r.N[2, part], weight(1, jj, 0, 512)) + bias
            sq = u * u
            t = jnp.tanh(0.7978845608028654 * (u + 0.044715 * sq * u))
            r.GP[jj, part] = 0.5 * (1.0 + t) + 0.5 * u * (1.0 - t * t) * (
                0.7978845608028654 * (1.0 + 3 * 0.044715 * sq))
            act = (0.5 * u * (1.0 + t)).astype(BF)
            r.ACT[jj, part] = act
            term = mm_nt(act, weight(1, jj, 512, 1024))
            total = term if total is None else total + term
        send_part(1, i, 256, total)

    loop(2, ffn)

    def running(part):
        mask = r.RN[part]
        return mask, mask * r.PR[part]

    def ffn_after(part):
        v = r.IN[part].astype(F32)
        diff = r.AS[part] + received(1, part) + param(DOWNB) - v
        r.DIF[part] = diff
        mask, run = running(part)
        lane = lax.broadcasted_iota(jnp.int32, (1, 128), 1)
        tally = jnp.where(lane == 1, run, jnp.where(lane == 2, mask, 0.0))
        r.SM[SCAL:SCAL + 1, 0:128] += jnp.sum(tally, axis=0, keepdims=True)
        return v + wide(run) * diff

    @pl.when(enc)
    def _():
        def memory_out(i):
            exchange_copy(1, i).wait()
            part = rows_of(i, 128)
            ln_to(1, part, 128, ffn_after(part))
            memory_copy(i).start()

        loop(4, memory_out)
        r.OB[...] = r.N[1]

    for q in range(4):
        got(r.COT.at[pl.ds(128 * q, 128)], rs["ct"].at[q])

    def halt_back(part, g):
        v = r.IN[part].astype(F32)
        mask, run = running(part)
        prob = r.PR[part]
        run = wide(run)
        d_aff = g * run
        r.DA[part] = d_aff
        r.FF[part] = d_aff.astype(BF)
        dot = jnp.sum(g * r.DIF[part], axis=-1, keepdims=True)
        zz = mask * dot * prob * (1.0 - prob)
        zw = wide(zz)
        r.DX[part] = g * (1.0 - run) + zw * param(HALTW)
        count(DOWNB, d_aff)
        count(HALTW, zw * v)
        lane = lax.broadcasted_iota(jnp.int32, (1, 128), 1)
        r.SM[SCAL:SCAL + 1, 0:128] += jnp.sum(jnp.where(lane == 0, zz, 0.0), axis=0, keepdims=True)

    def memory_grad_pass(i):
        for h in (0, 1):
            got(r.DM.at[half_rows(2 * i + h, c)], rs["dme"].at[2 * i + h, c])
            memory_grad_forward(2 * i + h).start()

    def memory_grad_in(i):
        def one(h):
            j = 2 * i + h
            got(r.DM.at[half_rows(j, sib)], rs["dme"].at[j, sib])
            part = rows_of(j, 128)
            n = r.COT[part].astype(F32) + r.DM[part].astype(F32)
            halt_back(part, ln_back(1, part, n))

        loop(2, one)
        pl.when(i == 0)(lambda: memory_grad_pass(1))

    def output_in(i):
        def one(h):
            exchange_copy(1, 2 * i + h).wait()
            part = rows_of(2 * i + h, 128)
            r.OB[part] = ffn_after(part).astype(BF)
            halt_back(part, r.COT[part].astype(F32))

        loop(2, one)

    @pl.when(enc)
    def _():
        flip(r.NT.at[2], r.N.at[2])
        flip(r.NT.at[0], r.N.at[0])
        memory_grad_pass(0)

    def ffn_back(i):
        pl.when(enc)(lambda: memory_grad_in(i))
        pl.when(dec)(lambda: output_in(i))
        part = rows_of(i, 256)
        total = None
        for jj in (0, 1):
            dp_ = mm(r.FF[part], weight(1, jj, 512, 1024)) * r.GP[jj, part]
            row = UPB + 2 * c + jj
            r.SM[pl.ds(row, 1), :] += jnp.sum(dp_, axis=0, keepdims=True)
            low = dp_.astype(BF)
            r.PB[jj, part] = low
            term = mm_nt(low, weight(1, jj, 0, 512))
            total = term if total is None else total + term
        send_part(0, i, 256, total)

    loop(2, ffn_back)
    for h in (0, 1):
        quarter = 2 * c + h
        put_or_keep(lambda h=h, quarter=quarter: (
            r.OB.at[rows_of(quarter, 128)], o_st.at[m], ss["os"].at[h], rs["os"].at[m], role, quarter))

    def ffn_weights(when):
        flip(r.LT, r.FF)
        for jj in (0, 1):
            outer(1, jj, 0, 512, r.NT.at[2], lambda: r.PB[jj])
            outer(1, jj, 512, 1024, r.LT, lambda: r.ACT[jj])
            reduce_first(1, jj, when)

    pl.when(enc)(lambda: ffn_weights(enc))

    def ffn_back_after(part):
        d = r.DA[part] + ln_back(2, part, received(0, part))
        r.DA[part] = d
        r.FB[part] = d.astype(BF)

    def heads_back(g, i):
        part = rows_of(i, 256)
        both_heads = mm(r.FB[part], both(g, 384, 512)).astype(BF)
        r.DH[0, part], r.DH[1, part] = both_heads[:, 0:128], both_heads[:, 128:256]

    def after_ffn_back(i):
        after_exchange(0, i, ffn_back_after)
        pl.when(enc)(lambda: heads_back(0, i))
        pl.when(dec)(lambda: heads_back(2, i))

    loop(2, after_ffn_back)

    @pl.when(dec)
    def _():
        attend_back(lambda jj: r.CQ[jj], r.CKV, 128, r.CKT, r.PX, 256, 0, 128)

        def memory_back(i):
            part = rows_of(i, 128)
            pairs = jnp.concatenate([r.DQ[0, part, 0:256], r.DQ[1, part, 0:256]], axis=1)
            r.DS[part] = mm_nt(pairs, both(2, 0, 256)).astype(BF)
            memory_grad_swap(i).start()

        loop(4, memory_back)

        def memory_grad_out(i):
            part = half_rows(i, c)
            got(r.DSR.at[part], rs["dmx"].at[i])
            r.DSO[part] = (r.DS[part].astype(F32) + r.DSR[part].astype(F32)).astype(BF)
            memory_grad_copy(i).start()

        loop(4, memory_grad_out)
        flip(r.NT.at[2], r.N.at[2])
        ffn_weights(dec)

        def query_back(i):
            part = rows_of(i, 256)
            asked = jnp.concatenate([r.DQ[0, part, 256:384], r.DQ[1, part, 256:384]], axis=1)
            send_part(1, i, 256, mm_nt(asked, both(2, 256, 384)))

        loop(2, query_back)
        flip(r.LT, r.FB)
        flip(r.NT.at[1], r.N.at[1])
        flip(r.MT, r.MEM)
        for jj in (0, 1):
            outer(2, jj, 0, 256, r.MT, lambda: r.DQ[jj, :, 0:256])
            outer(2, jj, 256, 384, r.NT.at[1], lambda: r.DQ[jj, :, 256:384])
            outer(2, jj, 384, 512, r.LT, lambda: r.HX[jj])
            reduce_first(2, jj, dec)

        def cross_back_after(part):
            d = r.DA[part] + ln_back(1, part, received(1, part))
            r.DA[part] = d
            r.FB[part] = d.astype(BF)

        def after_query_back(i):
            after_exchange(1, i, cross_back_after)
            heads_back(0, i)

        loop(2, after_query_back)

    flip(r.LT, r.FB)
    for jj in (0, 1):
        outer(0, jj, 384, 512, r.LT, lambda: r.HD[jj])
    attend_back(lambda jj: r.QKV[jj, :, 0:128], r.QKV, 256, r.KT, r.PA, 0, 128, 256)

    for jj in (0, 1):
        outer(0, jj, 0, 384, r.NT.at[0], lambda: r.DQ[jj])
        reduce_first(0, jj)

    def first_back(i):
        part = rows_of(i, 256)
        all_three = jnp.concatenate([r.DQ[0, part], r.DQ[1, part]], axis=1)
        send_part(2, i, 256, mm_nt(all_three, both(0, 0, 384)))

    loop(2, first_back)

    def first_back_after(part):
        d = r.DX[part] + r.DA[part] + ln_back(0, part, received(2, part))
        r.DXB[part] = d.astype(BF)

    loop(2, lambda i: after_exchange(2, i, first_back_after))
    for h in (0, 1):
        quarter = 2 * c + h
        put_or_keep(lambda h=h, quarter=quarter: (r.DXB.at[rows_of(quarter, 128)], o_dx.at[m], ss["od"].at[h], rs["od"].at[m], role, quarter))

    row_id = lax.broadcasted_iota(jnp.int32, (SMALL, T), 0)
    halves = jnp.logical_and(row_id >= UPB, row_id < DOWNB)
    r.SM2[...] = jnp.where(jnp.logical_or(halves, c == 0), r.SM[...], 0.0)
    for d in (1, 2, 3):
        put(lambda d=d: (r.SM2, r.LM1.at[d - 1], ss["m1"].at[d - 1], rs["m1"].at[d - 1], dev(zz=zs[d])))
    reduce_second(1)

    @pl.when(dec)
    def _():
        reduce_second(2)

    for d in range(3):
        got(r.LM1.at[d], rs["m1"].at[d])
    r.SM3[...] = r.SM2[...] + r.LM1[0] + r.LM1[1] + r.LM1[2]
    for d in (1, 2, 3):
        put(lambda d=d: (r.SM3, r.LM2.at[d - 1], ss["m2"].at[d - 1], rs["m2"].at[d - 1], dev(yy=ys[d])))

    reduce_second(0)
    reduce_third(1)

    @pl.when(dec)
    def _():
        reduce_third(2)

    for d in range(3):
        got(r.LM2.at[d], rs["m2"].at[d])
    r.SM[...] = r.SM3[...] + r.LM2[0] + r.LM2[1] + r.LM2[2]
    for k in range(4):
        put_or_keep(lambda k=k: (r.SM, o_sm.at[2 * m + c], ss["m3"].at[k], rs["m3"].at[2 * m + c], role, k))
    reduce_third(0)
    for k in range(4):
        got(o_sm.at[k], rs["m3"].at[k])
    for k in (0, 1):
        got(o_st.at[k], rs["os"].at[k])
        got(o_dx.at[k], rs["od"].at[k])
        for g in range(3):
            got(LC[g].at[k], rs["rc"].at[g, k])

    @pl.when(enc)
    def _():
        for i in range(4):
            memory_copy(i).wait_send()
            memory_grad_forward(i).wait_send()

    @pl.when(dec)
    def _():
        for i in range(4):
            memory_forward(i).wait_send()
            memory_grad_swap(i).wait_send()
            memory_grad_copy(i).wait_send()

    for end in ends:
        end()


def finish(st, dx, c0, c1, c2, small, o_st, o_dx, o_gain, o_shift, o_in, o_out, o_cross, o_up, o_upb, o_down, o_downb,
           o_haltw, o_haltb, o_act):
    o_st[...] = st[...]
    o_dx[...] = dx[...].astype(F32)
    both = c0[0].astype(F32) + c0[1].astype(F32)
    for k in range(3):
        o_in[k] = both[:, 128 * k:128 * k + 128]
    o_out[...] = both[:, 384:512]
    both = c1[0].astype(F32) + c1[1].astype(F32)
    o_up[...], o_down[...] = both[:, 0:512], both[:, 512:1024]
    both = c2[0].astype(F32) + c2[1].astype(F32)
    for k in (0, 1):
        o_cross[:, k, :] = both[:, 128 * k:128 * k + 128]
    total = small[0] + small[1] + small[2] + small[3]
    for k in range(3):
        o_gain[k] = total[GAIN + k:GAIN + k + 1]
        o_shift[k] = total[SHIFT + k:SHIFT + k + 1]
    for k in range(4):
        o_upb[:, 512 * k:512 * k + 512] = total[UPB + k:UPB + k + 1]
    o_downb[...] = total[DOWNB:DOWNB + 1]
    o_haltw[...] = total[HALTW:HALTW + 1]
    o_haltb[...] = total[SCAL:SCAL + 1, 0:1]
    ran, alive = total[SCAL:SCAL + 1, 1:2], total[SCAL:SCAL + 1, 2:3]
    o_act[...] = jnp.concatenate([ran / alive, 1.0 - alive / (32 * T)], axis=1)


def on_device(states, cotangent, halting, segments, norm_gain, norm_bias, attn_in, attn_out, cross, up_weight, up_bias,
              down_weight, down_bias, halt_weight, halt_bias):
    vm, anywhere = pl.BlockSpec(memory_space=pltpu.VMEM), pl.BlockSpec(memory_space=pl.ANY)
    arrived = pl.pallas_call(
        kernel,
        out_shape=[
            jax.ShapeDtypeStruct((2, 128, T), BF),
            jax.ShapeDtypeStruct((2, 128, T), BF),
            jax.ShapeDtypeStruct((2, 32, 512), BF),
            jax.ShapeDtypeStruct((2, 32, 1024), BF),
            jax.ShapeDtypeStruct((2, 32, 256), BF),
            jax.ShapeDtypeStruct((4, SMALL, T), F32),
        ],
        in_specs=[anywhere] * 2 + [vm] * 8 + [anywhere] * 2 + [vm] + [anywhere] * 2,
        out_specs=[anywhere] * 6,
        scratch_shapes=[pltpu.VMEM(*spec) for spec in SCRATCH.values()]
        + [pltpu.SemaphoreType.DMA(shape) for shape in SEMS.values() for _ in (0, 1)],
        compiler_params=pltpu.CompilerParams(
            collective_id=0, has_side_effects=True, vmem_limit_bytes=62 * 2**20),
        name="step",
    )(states[0], cotangent[0], halting[0], segments, jnp.transpose(norm_gain, (1, 0, 2)),
      jnp.transpose(norm_bias, (1, 0, 2)), up_bias.reshape(4, 1, T), down_bias, halt_weight,
      halt_bias.reshape(1, 1), jnp.transpose(attn_in[0], (1, 0, 2)), attn_out[0].T, cross[0], up_weight[0],
      down_weight[0].T)
    st, dx, gain, shift, g_in, g_out, g_cross, g_up, upb, g_down, downb, haltw, haltb, act = pl.pallas_call(
        finish,
        out_shape=[
            jax.ShapeDtypeStruct((2, 128, T), BF),
            jax.ShapeDtypeStruct((2, 128, T), F32),
            jax.ShapeDtypeStruct((3, 1, T), F32),
            jax.ShapeDtypeStruct((3, 1, T), F32),
            jax.ShapeDtypeStruct((3, 32, 128), F32),
            jax.ShapeDtypeStruct((32, 128), F32),
            jax.ShapeDtypeStruct((32, 2, 128), F32),
            jax.ShapeDtypeStruct((32, 512), F32),
            jax.ShapeDtypeStruct((1, 2048), F32),
            jax.ShapeDtypeStruct((32, 512), F32),
            jax.ShapeDtypeStruct((1, T), F32),
            jax.ShapeDtypeStruct((1, T), F32),
            jax.ShapeDtypeStruct((1, 1), F32),
            jax.ShapeDtypeStruct((1, 2), F32),
        ],
        in_specs=[vm] * 6,
        out_specs=[vm] * 14,
        name="finish",
    )(*arrived)
    return (
        st[None], dx[None], jnp.transpose(gain, (1, 0, 2)), jnp.transpose(shift, (1, 0, 2)),
        jnp.transpose(g_in, (1, 0, 2))[None], g_out.T[None], g_cross[None], g_up[None], upb, g_down.T[None], downb,
        haltw, haltb.reshape(1), act,
    )


def solution(mesh):
    split = (
        P("pipe", "dp", "mp", None), P("pipe", "dp", "mp", None), P("pipe", "dp", "mp"), P(None, "dp", None),
        P("pipe", None, None), P("pipe", None, None), P("pipe", "dp", None, "mp"), P("pipe", "mp", "dp"),
        P("pipe", "dp", None, "mp"), P("pipe", "dp", "mp"), P("pipe", None), P("pipe", "mp", "dp"),
        P("pipe", None), P("pipe", None), P("pipe"),
    )
    out = (
        P("pipe", "dp", "mp", None), P("pipe", "dp", "mp", None), P("pipe", None, None), P("pipe", None, None),
        P("pipe", "dp", None, "mp"), P("pipe", "mp", "dp"), P("pipe", "dp", None, "mp"), P("pipe", "dp", "mp"),
        P("pipe", None), P("pipe", "mp", "dp"), P("pipe", None), P("pipe", None), P("pipe"), P("pipe", None),
    )
    return jax.shard_map(on_device, mesh=mesh, in_specs=split, out_specs=out, check_vma=False)
```

```python
import jax
import jax.numpy as jnp
from jax import lax
from jax.experimental import pallas as pl
from jax.experimental.pallas import tpu as pltpu
from jax.sharding import PartitionSpec as P

MESH = pl.DeviceIdType.MESH
BF = jnp.bfloat16
F32 = jnp.float32
EPS = 1e-06
T = 512
SCALE = 0.125
WIDTHS = (512, 1024, 512)

GAIN, SHIFT, UPB, DOWNB, HALTW, SCAL = 0, 3, 6, 10, 11, 12
SMALL = 16

SCRATCH = dict(
    PSB=((32, 512), BF),
    PFB=((32, 1024), BF),
    PCB=((32, 256), BF),
    PK=((SMALL, T), F32),
    HB=((2, 16, 128), BF),
    HL=((4, 16, 128), BF),
    RN=((T, 128), F32),
    IN=((T, T), BF),
    COT=((T, T), BF),
    PSIB=((SMALL, T), F32),
    PV=((SMALL, T), F32),
    W0=((2, 4, 4, 32, 512), BF),
    W1=((2, 4, 4, 32, 1024), BF),
    W2=((2, 4, 4, 32, 512), BF),
    U=((3, T, T), F32),
    F=((3, T, 128), F32),
    N=((3, T, T), BF),
    QKV=((2, T, 384), BF),
    KT=((2, 128, T), BF),
    VT=((2, 128, T), BF),
    HD=((2, T, 128), BF),
    PA=((2, 2, T, T), BF),
    CQ=((2, T, 128), BF),
    CKV=((2, T, 256), BF),
    CKT=((2, 128, T), BF),
    CVT=((2, 128, T), BF),
    HX=((2, T, 128), BF),
    PX=((2, 2, T, T), BF),
    AS=((T, T), F32),
    DIF=((T, T), F32),
    GP=((2, T, T), F32),
    ACT=((2, T, T), BF),
    PB=((2, T, T), BF),
    DA=((T, T), F32),
    DX=((T, T), F32),
    FF=((T, T), BF),
    FB=((T, T), BF),
    XS=((3, T, T), BF),
    XR=((3, T, T), BF),
    BS=((T, T), F32),
    BX=((T, T), F32),
    MEM=((T, T), BF),
    DM=((T, T), BF),
    DS=((T, T), BF),
    DSR=((T, T), BF),
    DSO=((T, T), BF),
    DQ=((2, T, 384), BF),
    DH=((2, T, 128), BF),
    DSB=((2, T, T), BF),
    PR=((T, 128), F32),
    OB=((T, T), BF),
    DXB=((T, T), BF),
    G0=((2, 4, 4, 32, 512), BF),
    G1=((2, 4, 4, 32, 1024), BF),
    G2=((2, 4, 4, 32, 512), BF),
    RX0=((2, 2, 2, 32, 512), BF),
    RF0=((2, 2, 4, 32, 512), BF),
    RX1=((2, 2, 2, 32, 1024), BF),
    RF1=((2, 2, 4, 32, 1024), BF),
    RX2=((2, 2, 2, 32, 512), BF),
    RF2=((2, 2, 4, 32, 512), BF),
    SA0=((2, 4, 32, 512), BF),
    SA1=((2, 4, 32, 1024), BF),
    SA2=((2, 4, 32, 512), BF),
    LB1=((2, 3, 32, 1024), BF),
    LB2=((2, 3, 32, 512), BF),
    SB1=((2, 32, 1024), BF),
    SB2=((2, 32, 512), BF),
    SM=((SMALL, T), F32),
    LM1=((3, SMALL, T), F32),
    SM2=((SMALL, T), F32),
    LM2=((3, SMALL, T), F32),
    SM3=((SMALL, T), F32),
)

SEMS = dict(
    pp=(1,),
    g0=(2, 4),
    pf=(2,),
    pc=(2, 2),
    po=(2,),
    rk=(2, 2),
    st=(4,),
    hl=(4,),
    ct=(4,),
    lo=(6,),
    ga=(3, 3, 2, 3),
    ex=(3, 2),
    mem=(4, 2),
    mfw=(4,),
    dmx=(4,),
    dme=(4, 2),
    dmf=(4,),
    rs=(3, 2, 2, 6),
    rt=(3, 2, 3),
    rc=(3, 2),
    r0=(2, 4),
    os=(2,),
    od=(2,),
    m1=(3,),
    m2=(3,),
    m3=(4,),
)


def mm(a, b):
    return lax.dot_general(a, b, (((1,), (0,)), ((), ())), preferred_element_type=F32)


def mm_nt(a, b):
    return lax.dot_general(a, b, (((1,), (1,)), ((), ())), preferred_element_type=F32)


def mm_tn(a, b):
    return lax.dot_general(a, b, (((0,), (0,)), ((), ())), preferred_element_type=F32)


def rows_of(i, size):
    return pl.ds(pl.multiple_of(i * size, size), size)


def loop(count, body):
    lax.fori_loop(0, count, lambda i, _: (body(i), 0)[1], 0)


def wide(v):
    return jnp.concatenate([v, v, v, v], axis=1)


def mean(v):
    return jnp.mean(v, axis=-1, keepdims=True)


class Refs:
    pass


def kernel(*refs):
    (states, cot, halts, seg, gain, shift, upb, downb, haltw, haltb, w_in, w_out, w_cross, w_up, w_down,
     o_st, o_dx, o_c0, o_c1, o_c2, o_sm) = refs[:21]
    r = Refs()
    rest = refs[21:]
    for name, ref in zip(SCRATCH, rest):
        setattr(r, name, ref)
    rest = rest[len(SCRATCH):]
    ss, rs = {}, {}
    for k, name in enumerate(SEMS):
        ss[name], rs[name] = rest[2 * k], rest[2 * k + 1]
    W, G = (r.W0, r.W1, r.W2), (r.G0, r.G1, r.G2)
    RX, RF, SA = (r.RX0, r.RX1, r.RX2), (r.RF0, r.RF1, r.RF2), (r.SA0, r.SA1, r.SA2)
    LB, SB = (None, r.LB1, r.LB2), (None, r.SB1, r.SB2)
    LC = (o_c0, o_c1, o_c2)

    c = lax.axis_index("pipe")
    dp = lax.axis_index("dp")
    x = lax.axis_index("mp")
    y, z = dp // 4, lax.rem(dp, 4)
    dec = jnp.logical_or(x == 1, x == 2)
    enc = jnp.logical_not(dec)
    role = jnp.where(dec, 1, 0)
    m = x // 2
    sib = 1 - c
    pair = x + 1 - 2 * lax.rem(x, 2)
    zs = [lax.rem(z + d, 4) for d in range(4)]
    zb = [lax.rem(z + 4 - d, 4) for d in range(4)]
    ys = [lax.rem(y + d, 4) for d in range(4)]
    yb = [lax.rem(y + 4 - d, 4) for d in range(4)]

    def dev(core=c, yy=y, zz=z, xx=x):
        return (core, yy * 4 + zz, xx)

    def rdma(src, dst, ssem, rsem, to):
        return pltpu.make_async_remote_copy(
            src_ref=src, dst_ref=dst, send_sem=ssem, recv_sem=rsem, device_id=to, device_id_type=MESH
        )

    ends = []

    def put(what, when=None):
        rdma(*what()).start()

        def end():
            if when is None:
                rdma(*what()).wait_send()
            else:
                @pl.when(when)
                def _():
                    rdma(*what()).wait_send()

        ends.append(end)

    def put_or_keep(what, when=None):
        def away():
            core, xx = what()[4:]
            return jnp.logical_not(jnp.logical_and(core == c, xx == x))

        @pl.when(jnp.logical_not(away()))
        def _():
            src, dst, _, rsem, _, _ = what()
            pltpu.make_async_copy(src, dst, rsem).start()

        def remote():
            src, dst, ssem, rsem, core, xx = what()
            return rdma(src, dst, ssem, rsem, dev(core, xx=xx))

        @pl.when(away())
        def _():
            remote().start()

        def end():
            out = away()
            if when is not None:
                out = jnp.logical_and(out, when)

            @pl.when(out)
            def _():
                remote().wait_send()

        ends.append(end)

    def got(dst, rsem):
        pltpu.make_async_copy(dst, dst, rsem).wait()

    barrier = pltpu.get_barrier_semaphore()
    partners = [dev(zz=zs[d]) for d in (1, 2, 3)] + [dev(yy=ys[d]) for d in (1, 2, 3)]
    partners += [dev(core=sib, xx=lax.rem(x + d, 4)) for d in range(4)]
    partners += [dev(xx=lax.rem(x + d, 4)) for d in (1, 2, 3)]
    jj_me = lax.rem(x, 2)
    to_y = [jnp.where(jj_me == 0, y, ys[d]) for d in range(4)]
    to_z = [jnp.where(jj_me == 0, zs[d], z) for d in range(4)]
    for d in (1, 2, 3):
        partners.append(dev(core=role, zz=zb[d], xx=2 * c))
        partners.append(dev(core=role, yy=yb[d], xx=2 * c + 1))
        partners += [dev(core=x // 2, yy=to_y[d], zz=to_z[d], xx=home) for home in (c, 3 - c)]
    for to in partners:
        pl.semaphore_signal(barrier, inc=1, device_id=to, device_id_type=MESH)

    staged = [
        (w_in.at[0], r.PSB.at[:, pl.ds(0, 128)]), (w_in.at[1], r.PSB.at[:, pl.ds(128, 128)]),
        (w_in.at[2], r.PSB.at[:, pl.ds(256, 128)]), (w_out, r.PSB.at[:, pl.ds(384, 128)]),
        (w_up, r.PFB.at[:, pl.ds(0, 512)]), (w_down, r.PFB.at[:, pl.ds(512, 512)])]
    staged = [pltpu.make_async_copy(a, b, rs["lo"].at[k]) for k, (a, b) in enumerate(staged)]
    for copy in staged:
        copy.start()
    r.PK[GAIN:GAIN + 3] = gain[:, 0, :]
    r.PK[SHIFT:SHIFT + 3] = shift[:, 0, :]
    r.PK[UPB:UPB + 4] = upb[:, 0, :]
    r.PK[DOWNB:DOWNB + 1] = downb[...]
    r.PK[HALTW:HALTW + 1] = haltw[...]
    r.PK[SCAL:SCAL + 1] = jnp.broadcast_to(haltb[...], (1, T))
    r.PK[SCAL + 1:SMALL] = jnp.zeros((SMALL - SCAL - 1, T), F32)
    for k in (0, 1):
        r.HB[k] = jnp.broadcast_to(halts[k:k + 1].astype(F32), (16, 128)).astype(BF)
    crossed = w_cross[...].astype(F32)
    for k in (0, 1):
        r.PCB[:, 128 * k:128 * k + 128] = crossed[:, k, :].astype(BF)
    for copy in staged:
        copy.wait()
    pl.semaphore_wait(barrier, len(partners))

    homes = (c, 3 - c)

    def gather_first(g):
        for d in (1, 2, 3):
            put(lambda d=d: (W[g].at[0, y, z], W[g].at[0, y, z], ss["ga"].at[g, 0, 0, d - 1], rs["ga"].at[g, 0, 0, d - 1], dev(zz=zs[d])), dec if g == 2 else None)
            put(lambda d=d: (W[g].at[1, y, z], W[g].at[1, y, z], ss["ga"].at[g, 0, 1, d - 1], rs["ga"].at[g, 0, 1, d - 1], dev(yy=ys[d])), dec if g == 2 else None)

    low_half, high_half = pl.ds(0, 2), pl.ds(2, 2)

    def block(ref, jj, at, half=None):
        if jj == 0:
            return ref.at[0, at] if half is None else ref.at[0, at, half]
        return ref.at[1, :, at] if half is None else ref.at[1, half, at]

    def along(jj, d):
        if jj == 0:
            return ys[d % 4], dev(yy=ys[d % 4])
        return zs[d % 4], dev(zz=zs[d % 4])

    def gather_second(g):
        for d in range(4):
            if g == 0:
                got(W[g].at[0, y, zb[d]], rs["g0"].at[0, d])
                got(W[g].at[1, yb[d], z], rs["g0"].at[1, d])
            elif d > 0:
                got(W[g].at[0, y, zb[d]], rs["ga"].at[g, 0, 0, d - 1])
                got(W[g].at[1, yb[d], z], rs["ga"].at[g, 0, 1, d - 1])
        for jj in (0, 1):
            for k, d in ((0, 1), (1, 3)):
                def what(jj=jj, k=k, d=d):
                    mine = block(W[g], jj, along(jj, 0)[0])
                    return mine, mine, ss["ga"].at[g, 1, jj, k], rs["ga"].at[g, 1, jj, k], along(jj, d)[1]

                put(what, dec if g == 2 else None)

    def gather_pass(g):
        for jj in (0, 1):
            for k, d in ((0, 1), (1, 3)):
                behind = along(jj, 4 - d)[0]
                got(block(W[g], jj, behind), rs["ga"].at[g, 1, jj, k])

                def what(jj=jj, k=k, d=d):
                    part = block(W[g], jj, along(jj, 4 - d)[0], (low_half, high_half)[k])
                    return part, part, ss["ga"].at[g, 2, jj, k], rs["ga"].at[g, 2, jj, k], along(jj, d)[1]

                put(what, dec if g == 2 else None)

    def gather_done(g):
        for jj in (0, 1):
            for k in (0, 1):
                got(block(W[g], jj, along(jj, 2)[0], (low_half, high_half)[k]), rs["ga"].at[g, 2, jj, k])

    def reduce_first(g, jj, h=0, when=None):
        cols = pl.ds(512 * h, 512)
        for k, d in ((0, 1), (1, 3)):
            halves = (low_half, high_half)

            def far(k=k, d=d):
                return (block(G[g].at[..., cols], jj, along(jj, 2)[0], halves[k]), RX[g].at[jj, k, :, :, cols],
                        ss["rs"].at[g, h, jj, k], rs["rs"].at[g, h, jj, k], along(jj, d)[1])

            put(far, when)
        for k, d in ((0, 1), (1, 3)):
            def near(k=k, d=d):
                return (block(G[g].at[..., cols], jj, along(jj, d)[0], halves[1 - k]),
                        RF[g].at[jj, k, halves[1 - k], :, cols],
                        ss["rs"].at[g, h, jj, 2 + k], rs["rs"].at[g, h, jj, 2 + k], along(jj, d)[1])

            put(near, when)

    def reduce_pass(g, h=0, when=None):
        cols = pl.ds(512 * h, 512)
        for jj in (0, 1):
            for k, d in ((0, 1), (1, 3)):
                got(RX[g].at[jj, k, :, :, cols], rs["rs"].at[g, h, jj, k])
                at = along(jj, d)[0]
                own = G[g][0, at, 2 * k:2 * k + 2, :, cols] if jj == 0 else G[g][1, 2 * k:2 * k + 2, at, :, cols]
                RX[g][jj, k, :, :, cols] = (own.astype(F32) + RX[g][jj, k, :, :, cols].astype(F32)).astype(BF)

                def what(jj=jj, k=k, d=d):
                    return (RX[g].at[jj, k, :, :, cols], RF[g].at[jj, k, (low_half, high_half)[k], :, cols],
                            ss["rs"].at[g, h, jj, 4 + k], rs["rs"].at[g, h, jj, 4 + k], along(jj, d)[1])

                put(what, when)

    def reduce_second(g):
        for jj in (0, 1):
            for k in (0, 1):
                for h in (0, 1) if g == 1 else (0,):
                    cols = pl.ds(512 * h, 512)
                    halves = (low_half, high_half)
                    got(RF[g].at[jj, k, halves[1 - k], :, cols], rs["rs"].at[g, h, jj, 2 + k])
                    got(RF[g].at[jj, k, halves[k], :, cols], rs["rs"].at[g, h, jj, 4 + k])

            def add(i):
                own = G[g][0, y, i] if jj == 0 else G[g][1, i, z]
                total = own.astype(F32) + RF[g][jj, 0, i].astype(F32) + RF[g][jj, 1, i].astype(F32)
                SA[g][jj, i] = total.astype(BF)

            loop(4, add)
            if g == 0:
                put_or_keep(lambda jj=jj: (
                    SA[0].at[jj, z if jj == 0 else y], o_c0.at[m, 0], ss["r0"].at[jj, 0], rs["r0"].at[m, 0],
                    role, 2 * c + jj))
                for d in (1, 2, 3):
                    put(lambda jj=jj, d=d: (
                        SA[0].at[jj, zs[d] if jj == 0 else ys[d]], o_c0.at[m, d], ss["r0"].at[jj, d],
                        rs["r0"].at[m, d],
                        dev(core=role, zz=zs[d], xx=2 * c) if jj == 0 else dev(core=role, yy=ys[d], xx=2 * c + 1)))
            else:
                for d in (1, 2, 3):
                    def what(d=d, jj=jj):
                        src, to = ((SA[g].at[0, zs[d]], dev(zz=zs[d])) if jj == 0 else
                                   (SA[g].at[1, ys[d]], dev(yy=ys[d])))
                        return (src, LB[g].at[jj, d - 1], ss["rt"].at[g, jj, d - 1],
                                rs["rt"].at[g, jj, d - 1], to)

                    put(what, dec if g == 2 else None)

    def reduce_third(g):
        for jj in (0, 1):
            for d in (1, 2, 3):
                got(LB[g].at[jj, d - 1], rs["rt"].at[g, jj, d - 1])
            total = (SA[g][0, z] if jj == 0 else SA[g][1, y]).astype(F32)
            for d in range(3):
                total = total + LB[g][jj, d].astype(F32)
            SB[g][jj] = total.astype(BF)
            if g == 2:
                for k in (0, 1):
                    put_or_keep(lambda jj=jj, k=k: (
                        SB[g].at[jj, :, pl.ds(256 * k, 256)], LC[g].at[m], ss["rk"].at[k, jj], rs["rc"].at[g, m],
                        k, 2 * c + jj), dec)
            else:
                put_or_keep(lambda jj=jj: (
                    SB[g].at[jj], LC[g].at[m], ss["rc"].at[g, jj], rs["rc"].at[g, m], role, 2 * c + jj))

    def half_rows(i, core):
        return pl.ds(pl.multiple_of(256 * (i // 2) + 128 * core + 64 * lax.rem(i, 2), 64), 64)

    def memory_copy(i):
        part = half_rows(i, c)
        return rdma(r.N.at[1, part], r.MEM.at[part], ss["mem"].at[i, 0], rs["mem"].at[i, c], dev(xx=pair))

    def memory_forward(i):
        part = half_rows(i, c)
        return rdma(r.MEM.at[part], r.MEM.at[part], ss["mfw"].at[i], rs["mem"].at[i, c], dev(core=sib))

    def memory_grad_swap(i):
        part = half_rows(i, sib)
        return rdma(r.DS.at[part], r.DSR.at[part], ss["dmx"].at[i], rs["dmx"].at[i], dev(core=sib))

    def memory_grad_copy(i):
        part = half_rows(i, c)
        return rdma(r.DSO.at[part], r.DM.at[part], ss["dme"].at[i, 0], rs["dme"].at[i, c], dev(xx=pair))

    def memory_grad_forward(i):
        part = half_rows(i, c)
        return rdma(r.DM.at[part], r.DM.at[part], ss["dmf"].at[i], rs["dme"].at[i, c], dev(core=sib))

    def exchange_copy(k, i):
        part = rows_of(i, 256)
        return rdma(r.XS.at[k, part], r.XR.at[k, part], ss["ex"].at[k, i], rs["ex"].at[k, i], dev(core=sib))

    for d in range(4):
        for k in (0, 1):
            if d == 0:
                put_or_keep(lambda k=k: (
                    r.PSB, r.W0.at[jj_me, y, z], ss["g0"].at[k, 0], rs["g0"].at[jj_me, 0], x // 2, homes[k]))
            else:
                put(lambda k=k, d=d: (
                    r.PSB, r.W0.at[jj_me, y, z], ss["g0"].at[k, d], rs["g0"].at[jj_me, d],
                    dev(core=x // 2, yy=to_y[d], zz=to_z[d], xx=homes[k])))
    for k in (0, 1):
        put_or_keep(lambda k=k: (
            r.PFB, r.W1.at[jj_me, y, z], ss["pf"].at[k], rs["pf"].at[jj_me], x // 2, homes[k]))
    put(lambda: (r.PK, r.PSIB, ss["pp"].at[0], rs["pp"].at[0], dev(core=sib)))
    r.SM[...] = jnp.zeros((SMALL, T), F32)
    for jj in (0, 1):
        got(r.W1.at[jj, y, z], rs["pf"].at[jj])
    gather_first(1)
    for k in (0, 1):
        for core in (0, 1):
            put_or_keep(lambda k=k, core=core: (
                states.at[k], r.IN.at[rows_of(x, 128)], ss["st"].at[2 * k + core], rs["st"].at[x], core, homes[k]))
            put_or_keep(lambda k=k, core=core: (
                r.HB.at[k], r.HL.at[x], ss["hl"].at[2 * k + core], rs["hl"].at[x], core, homes[k]))
    gather_second(0)
    for k in (0, 1):
        put_or_keep(lambda k=k: (
            r.PCB, r.W2.at[jj_me, y, z, :, pl.ds(pl.multiple_of(256 * c, 256), 256)], ss["po"].at[k],
            rs["pc"].at[jj_me, c], x // 2, k + 1))
    gather_second(1)
    gather_pass(0)
    for k in (0, 1):
        for core in (0, 1):
            put_or_keep(lambda k=k, core=core: (
                cot.at[k], r.COT.at[rows_of(x, 128)], ss["ct"].at[2 * k + core], rs["ct"].at[x], core, homes[k]))
    got(r.PSIB, rs["pp"].at[0])
    r.PV[...] = jnp.where(c == role, r.PK[...], r.PSIB[...])
    for q in range(4):
        got(r.IN.at[pl.ds(128 * q, 128)], rs["st"].at[q])
        got(r.HL.at[q], rs["hl"].at[q])

    def param(row):
        return r.PV[pl.ds(row, 1), :]

    def ln_to(li, part, size, v):
        center = v - mean(v)
        factor = lax.rsqrt(mean(center * center) + EPS)
        unit = center * factor
        normed = unit * param(GAIN + li) + param(SHIFT + li)
        r.U[li, part] = unit
        r.F[li, part] = jnp.broadcast_to(factor, (size, 128))
        r.N[li, part] = normed.astype(BF)

    def count(row, v):
        r.SM[pl.ds(row, 1), :] += jnp.sum(v, axis=0, keepdims=True)

    def ln_back(li, part, n):
        unit, factor = r.U[li, part], wide(r.F[li, part])
        scaled = n * param(GAIN + li)
        count(GAIN + li, n * unit)
        count(SHIFT + li, n)
        return factor * (scaled - mean(scaled) - unit * mean(scaled * unit))

    def weight(g, jj, lo, hi):
        return W[g][jj, :, :, :, lo:hi].reshape(T, hi - lo)

    def both(g, lo, hi):
        return jnp.concatenate([weight(g, 0, lo, hi), weight(g, 1, lo, hi)], axis=1)

    def send_part(k, i, value):
        r.XS[k, rows_of(i, 256)] = value.astype(BF)
        exchange_copy(k, i).start()

    def received(k, part):
        return r.XS[k, part].astype(F32) + r.XR[k, part].astype(F32)

    def after_exchange(k, i, body):
        exchange_copy(k, i).wait()
        body(rows_of(i, 256))

    low_lane = lax.broadcasted_iota(jnp.int32, (1, 128), 1) < 64

    def head_part(v, hh):
        return jnp.where(low_lane if hh == 0 else jnp.logical_not(low_lane), v, jnp.zeros_like(v))

    def attend(q_of, kv, k_at, vt, bias, probs, heads):
        for jj in (0, 1):
            q, keys = q_of(jj), kv[jj, :, k_at:k_at + 128]
            outs = []
            for hh in (0, 1):
                s = mm_nt(keys, head_part(q, hh)) + bias[...]
                e = jnp.exp(s - jnp.max(s, axis=0, keepdims=True))
                w = (e * (1.0 / jnp.sum(e, axis=0, keepdims=True))).astype(BF)
                probs[jj, hh] = w
                outs.append(mm(vt[jj, 64 * hh:64 * hh + 64, :], w))
            heads[jj] = jnp.concatenate(outs, axis=0).T.astype(BF)

    def attend_back(q_of, kv, v_at, kt, probs, dq_at, dk_at, dv_at):
        for jj in (0, 1):
            q, o, values = q_of(jj), r.DH[jj], kv[jj, :, v_at:v_at + 128]
            for hh in (0, 1):
                w = probs[jj, hh].astype(F32)
                wd = w * mm_nt(values, head_part(o, hh))
                delta = jnp.sum(wd, axis=0, keepdims=True)
                r.DSB[hh] = (wd - w * delta).astype(BF)
            dks = [mm(r.DSB[hh], q) for hh in (0, 1)]
            dvs = [mm(probs[jj, hh], o) for hh in (0, 1)]
            dqs = [mm(kt[jj, 64 * hh:64 * hh + 64, :], r.DSB[hh]) for hh in (0, 1)]
            r.DQ[jj, :, dk_at:dk_at + 128] = jnp.where(low_lane, dks[0], dks[1]).astype(BF)
            r.DQ[jj, :, dv_at:dv_at + 128] = jnp.where(low_lane, dvs[0], dvs[1]).astype(BF)
            r.DQ[jj, :, dq_at:dq_at + 128] = (jnp.concatenate(dqs, axis=0).T * SCALE).astype(BF)

    def outer(g, jj, lo, hi, left, right):
        G[g][jj, :, :, :, lo:hi] = mm_tn(left[...], right()).astype(BF).reshape(4, 4, 32, hi - lo)

    def first(i):
        part = rows_of(i, 256)
        v = r.IN[part].astype(F32)
        ln_to(0, part, 256, v)
        logit = jnp.sum(v * param(HALTW), axis=-1, keepdims=True) + param(SCAL)[:, 0:1]
        r.PR[part] = jnp.broadcast_to(jax.nn.sigmoid(logit), (256, 128))
        for h in (0, 1):
            r.RN[rows_of(2 * i + h, 128)] = mm_tn(r.HL[2 * i + h], jnp.full((16, 128), 1.0 / 16.0, BF))

    loop(2, first)

    docs = lax.broadcasted_iota(jnp.int32, (16, T), 0)
    seg_src, seg_tgt = seg[0, pl.ds(m, 1), :], seg[1, pl.ds(m, 1), :]
    own_src = jnp.where(docs == seg_src, 1.0, 0.0).astype(BF)
    own_tgt = jnp.where(docs == seg_tgt, 1.0, 0.0).astype(BF)
    own_self = jnp.where(enc, own_src, own_tgt)
    k_at = lax.broadcasted_iota(jnp.int32, (T, T), 1)
    q_at = lax.broadcasted_iota(jnp.int32, (T, T), 0)
    reach = jnp.where(enc, T, 0)
    same = jnp.logical_and(mm_tn(own_self, own_self) > 0.5, q_at <= k_at + reach)
    r.BS[...] = jnp.where(same, 0.0, -1e30)

    @pl.when(dec)
    def _():
        r.BX[...] = jnp.where(mm_tn(own_src, own_tgt) > 0.5, 0.0, -1e30)

    @pl.when(dec)
    def _():
        for jj in (0, 1):
            for k in (0, 1):
                got(r.W2.at[jj, y, z, :, pl.ds(256 * k, 256)], rs["pc"].at[jj, k])
        gather_first(2)

    gather_done(0)

    for jj in (0, 1):
        three = mm(r.N[0], weight(0, jj, 0, 384))
        r.QKV[jj, :, 0:128] = (three[:, 0:128] * SCALE).astype(BF)
        r.QKV[jj, :, 128:384] = three[:, 128:384].astype(BF)
        r.KT[jj] = three[:, 128:256].T.astype(BF)
        r.VT[jj] = three[:, 256:384].T.astype(BF)

    gather_pass(1)
    attend(lambda jj: r.QKV[jj, :, 0:128], r.QKV, 128, r.VT, r.BS, r.PA, r.HD)

    @pl.when(dec)
    def _():
        gather_second(2)

    def self_out(i):
        part = rows_of(i, 256)
        heads = jnp.concatenate([r.HD[0, part], r.HD[1, part]], axis=1)
        send_part(0, i, mm_nt(heads, both(0, 384, 512)))

    loop(2, self_out)
    second = jnp.where(enc, 2, 1)

    def self_after(part):
        v = r.IN[part].astype(F32) + received(0, part)
        r.AS[part] = v
        ln_to(second, part, 256, v)

    @pl.when(dec)
    def _():
        gather_pass(2)
        gather_done(2)
        loop(2, lambda i: after_exchange(0, i, self_after))
        for jj in (0, 1):
            def ask(i):
                part = rows_of(i, 256)
                r.CQ[jj, part] = (mm(r.N[1, part], weight(2, jj, 256, 384)) * SCALE).astype(BF)

            loop(2, ask)

        def memory_in(i):
            for p in (0, 1):
                got(r.MEM.at[half_rows(2 * i + p, c)], rs["mem"].at[2 * i + p, c])
                memory_forward(2 * i + p).start()
            for p in (0, 1):
                got(r.MEM.at[half_rows(2 * i + p, sib)], rs["mem"].at[2 * i + p, sib])
            part = rows_of(i, 256)
            for jj in (0, 1):
                pairs = mm(r.MEM[part], weight(2, jj, 0, 256))
                r.CKV[jj, part] = pairs.astype(BF)
                r.CKT[jj, :, part] = pairs[:, 0:128].T.astype(BF)
                r.CVT[jj, :, part] = pairs[:, 128:256].T.astype(BF)

        loop(2, memory_in)
        attend(lambda jj: r.CQ[jj], r.CKV, 0, r.CVT, r.BX, r.PX, r.HX)

        def cross_out(i):
            part = rows_of(i, 256)
            heads = jnp.concatenate([r.HX[0, part], r.HX[1, part]], axis=1)
            send_part(2, i, mm_nt(heads, both(2, 384, 512)))

        loop(2, cross_out)

    gather_done(1)

    def cross_after(part):
        v = r.AS[part] + received(2, part)
        r.AS[part] = v
        ln_to(2, part, 256, v)

    def ffn(i):
        pl.when(enc)(lambda: after_exchange(0, i, self_after))
        pl.when(dec)(lambda: after_exchange(2, i, cross_after))
        part = rows_of(i, 256)
        total = None
        for jj in (0, 1):
            bias = r.PV[pl.ds(UPB + 2 * c + jj, 1), :]
            u = mm(r.N[2, part], weight(1, jj, 0, 512)) + bias
            sq = u * u
            t = jnp.tanh(0.7978845608028654 * (u + 0.044715 * sq * u))
            r.GP[jj, part] = 0.5 * (1.0 + t) + 0.5 * u * (1.0 - t * t) * (
                0.7978845608028654 * (1.0 + 3 * 0.044715 * sq))
            act = (0.5 * u * (1.0 + t)).astype(BF)
            r.ACT[jj, part] = act
            term = mm_nt(act, weight(1, jj, 512, 1024))
            total = term if total is None else total + term
        send_part(1, i, total)

    loop(2, ffn)

    def running(part):
        mask = r.RN[part]
        return mask, mask * r.PR[part]

    def ffn_after(part):
        v = r.IN[part].astype(F32)
        diff = r.AS[part] + received(1, part) + param(DOWNB) - v
        r.DIF[part] = diff
        mask, run = running(part)
        lane = lax.broadcasted_iota(jnp.int32, (1, 128), 1)
        tally = jnp.where(lane == 1, run, jnp.where(lane == 2, mask, 0.0))
        r.SM[SCAL:SCAL + 1, 0:128] += jnp.sum(tally, axis=0, keepdims=True)
        return v + wide(run) * diff

    @pl.when(enc)
    def _():
        def memory_out(i):
            exchange_copy(1, i).wait()
            part = rows_of(i, 256)
            ln_to(1, part, 256, ffn_after(part))
            for p in (0, 1):
                memory_copy(2 * i + p).start()

        loop(2, memory_out)
        r.OB[...] = r.N[1]

    for q in range(4):
        got(r.COT.at[pl.ds(128 * q, 128)], rs["ct"].at[q])

    def halt_back(part, g):
        v = r.IN[part].astype(F32)
        mask, run = running(part)
        prob = r.PR[part]
        run = wide(run)
        d_aff = g * run
        r.DA[part] = d_aff
        r.FF[part] = d_aff.astype(BF)
        dot = jnp.sum(g * r.DIF[part], axis=-1, keepdims=True)
        zz = mask * dot * prob * (1.0 - prob)
        zw = wide(zz)
        r.DX[part] = g * (1.0 - run) + zw * param(HALTW)
        count(DOWNB, d_aff)
        count(HALTW, zw * v)
        lane = lax.broadcasted_iota(jnp.int32, (1, 128), 1)
        r.SM[SCAL:SCAL + 1, 0:128] += jnp.sum(jnp.where(lane == 0, zz, 0.0), axis=0, keepdims=True)

    def memory_grad_pass(i):
        for h in (0, 1):
            got(r.DM.at[half_rows(2 * i + h, c)], rs["dme"].at[2 * i + h, c])
            memory_grad_forward(2 * i + h).start()

    def memory_grad_in(i):
        for h in (0, 1):
            got(r.DM.at[half_rows(2 * i + h, sib)], rs["dme"].at[2 * i + h, sib])
        part = rows_of(i, 256)
        n = r.COT[part].astype(F32) + r.DM[part].astype(F32)
        halt_back(part, ln_back(1, part, n))
        pl.when(i == 0)(lambda: memory_grad_pass(1))

    def output_in(i):
        exchange_copy(1, i).wait()
        part = rows_of(i, 256)
        r.OB[part] = ffn_after(part).astype(BF)
        halt_back(part, r.COT[part].astype(F32))

    def down_weights():
        for jj in (0, 1):
            outer(1, jj, 512, 1024, r.FF, lambda: r.ACT[jj])

    def up_weights():
        for jj in (0, 1):
            outer(1, jj, 0, 512, r.N.at[2], lambda: r.PB[jj])

    @pl.when(enc)
    def _():
        memory_grad_pass(0)
        loop(2, memory_grad_in)
        down_weights()
        for jj in (0, 1):
            reduce_first(1, jj, 1, enc)

    def ffn_back(i):
        pl.when(dec)(lambda: output_in(i))
        part = rows_of(i, 256)
        total = None
        for jj in (0, 1):
            dp_ = mm(r.FF[part], weight(1, jj, 512, 1024)) * r.GP[jj, part]
            row = UPB + 2 * c + jj
            r.SM[pl.ds(row, 1), :] += jnp.sum(dp_, axis=0, keepdims=True)
            low = dp_.astype(BF)
            r.PB[jj, part] = low
            term = mm_nt(low, weight(1, jj, 0, 512))
            total = term if total is None else total + term
        send_part(0, i, total)

    loop(2, ffn_back)
    for h in (0, 1):
        quarter = 2 * c + h
        put_or_keep(lambda h=h, quarter=quarter: (
            r.OB.at[rows_of(quarter, 128)], o_st.at[m], ss["os"].at[h], rs["os"].at[m], role, quarter))

    @pl.when(enc)
    def _():
        up_weights()
        for jj in (0, 1):
            reduce_first(1, jj, 0, enc)
        reduce_pass(1, 1, enc)

    def ffn_back_after(part):
        d = r.DA[part] + ln_back(2, part, received(0, part))
        r.DA[part] = d
        r.FB[part] = d.astype(BF)

    def heads_back(g, i):
        part = rows_of(i, 256)
        both_heads = mm(r.FB[part], both(g, 384, 512)).astype(BF)
        r.DH[0, part], r.DH[1, part] = both_heads[:, 0:128], both_heads[:, 128:256]

    def after_ffn_back(i):
        after_exchange(0, i, ffn_back_after)
        pl.when(enc)(lambda: heads_back(0, i))
        pl.when(dec)(lambda: heads_back(2, i))

    loop(2, after_ffn_back)

    @pl.when(dec)
    def _():
        attend_back(lambda jj: r.CQ[jj], r.CKV, 128, r.CKT, r.PX, 256, 0, 128)

        def memory_back(i):
            part = rows_of(i, 256)
            pairs = jnp.concatenate([r.DQ[0, part, 0:256], r.DQ[1, part, 0:256]], axis=1)
            r.DS[part] = mm_nt(pairs, both(2, 0, 256)).astype(BF)
            for p in (0, 1):
                memory_grad_swap(2 * i + p).start()

        loop(2, memory_back)

        def memory_grad_out(i):
            part = half_rows(i, c)
            got(r.DSR.at[part], rs["dmx"].at[i])
            r.DSO[part] = (r.DS[part].astype(F32) + r.DSR[part].astype(F32)).astype(BF)
            memory_grad_copy(i).start()

        loop(4, memory_grad_out)
        down_weights()
        for jj in (0, 1):
            reduce_first(1, jj, 1, dec)
        up_weights()
        for jj in (0, 1):
            reduce_first(1, jj, 0, dec)

        def query_back(i):
            part = rows_of(i, 256)
            asked = jnp.concatenate([r.DQ[0, part, 256:384], r.DQ[1, part, 256:384]], axis=1)
            send_part(1, i, mm_nt(asked, both(2, 256, 384)))

        loop(2, query_back)
        for jj in (0, 1):
            outer(2, jj, 0, 256, r.MEM, lambda: r.DQ[jj, :, 0:256])
            outer(2, jj, 256, 384, r.N.at[1], lambda: r.DQ[jj, :, 256:384])
            outer(2, jj, 384, 512, r.FB, lambda: r.HX[jj])
            reduce_first(2, jj, 0, dec)

        def cross_back_after(part):
            d = r.DA[part] + ln_back(1, part, received(1, part))
            r.DA[part] = d
            r.FB[part] = d.astype(BF)

        reduce_pass(1, 1, dec)

        def after_query_back(i):
            after_exchange(1, i, cross_back_after)
            heads_back(0, i)

        loop(2, after_query_back)

    for jj in (0, 1):
        outer(0, jj, 384, 512, r.FB, lambda: r.HD[jj])
    attend_back(lambda jj: r.QKV[jj, :, 0:128], r.QKV, 256, r.KT, r.PA, 0, 128, 256)

    reduce_pass(1, 0)
    for jj in (0, 1):
        outer(0, jj, 0, 384, r.N.at[0], lambda: r.DQ[jj])
        reduce_first(0, jj)

    def first_back(i):
        part = rows_of(i, 256)
        all_three = jnp.concatenate([r.DQ[0, part], r.DQ[1, part]], axis=1)
        send_part(2, i, mm_nt(all_three, both(0, 0, 384)))

    loop(2, first_back)

    @pl.when(dec)
    def _():
        reduce_pass(2, 0, dec)

    def first_back_after(part):
        d = r.DX[part] + r.DA[part] + ln_back(0, part, received(2, part))
        r.DXB[part] = d.astype(BF)

    loop(2, lambda i: after_exchange(2, i, first_back_after))
    for h in (0, 1):
        quarter = 2 * c + h
        put_or_keep(lambda h=h, quarter=quarter: (r.DXB.at[rows_of(quarter, 128)], o_dx.at[m], ss["od"].at[h], rs["od"].at[m], role, quarter))

    row_id = lax.broadcasted_iota(jnp.int32, (SMALL, T), 0)
    halves = jnp.logical_and(row_id >= UPB, row_id < DOWNB)
    r.SM2[...] = jnp.where(jnp.logical_or(halves, c == 0), r.SM[...], 0.0)
    for d in (1, 2, 3):
        put(lambda d=d: (r.SM2, r.LM1.at[d - 1], ss["m1"].at[d - 1], rs["m1"].at[d - 1], dev(zz=zs[d])))
    reduce_pass(0)
    for d in range(3):
        got(r.LM1.at[d], rs["m1"].at[d])
    r.SM3[...] = r.SM2[...] + r.LM1[0] + r.LM1[1] + r.LM1[2]
    for d in (1, 2, 3):
        put(lambda d=d: (r.SM3, r.LM2.at[d - 1], ss["m2"].at[d - 1], rs["m2"].at[d - 1], dev(yy=ys[d])))

    reduce_second(1)

    @pl.when(dec)
    def _():
        reduce_second(2)

    reduce_second(0)
    for d in range(3):
        got(r.LM2.at[d], rs["m2"].at[d])
    r.SM[...] = r.SM3[...] + r.LM2[0] + r.LM2[1] + r.LM2[2]
    for k in range(4):
        put_or_keep(lambda k=k: (r.SM, o_sm.at[2 * m + c], ss["m3"].at[k], rs["m3"].at[2 * m + c], role, k))
    reduce_third(1)

    @pl.when(dec)
    def _():
        reduce_third(2)

    for k in range(4):
        got(o_sm.at[k], rs["m3"].at[k])
    for k in (0, 1):
        got(o_st.at[k], rs["os"].at[k])
        got(o_dx.at[k], rs["od"].at[k])
        for g in (1, 2):
            got(LC[g].at[k], rs["rc"].at[g, k])
        for d in range(4):
            got(o_c0.at[k, d], rs["r0"].at[k, d])

    @pl.when(enc)
    def _():
        for i in range(4):
            memory_copy(i).wait_send()
            memory_grad_forward(i).wait_send()

    @pl.when(dec)
    def _():
        for i in range(4):
            memory_forward(i).wait_send()
            memory_grad_swap(i).wait_send()
            memory_grad_copy(i).wait_send()

    for end in ends:
        end()


def finish(st, dx, c0, c1, c2, small, o_st, o_dx, o_gain, o_shift, o_in, o_out, o_cross, o_up, o_upb, o_down, o_downb,
           o_haltw, o_haltb, o_act):
    o_st[...] = st[...]
    o_dx[...] = dx[...].astype(F32)
    both = c0[0, 0].astype(F32)
    for k in range(1, 8):
        both = both + c0[k // 4, k % 4].astype(F32)
    for k in range(3):
        o_in[k] = both[:, 128 * k:128 * k + 128]
    o_out[...] = both[:, 384:512]
    both = c1[0].astype(F32) + c1[1].astype(F32)
    o_up[...], o_down[...] = both[:, 0:512], both[:, 512:1024]
    both = c2[0].astype(F32) + c2[1].astype(F32)
    for k in (0, 1):
        o_cross[:, k, :] = both[:, 128 * k:128 * k + 128]
    total = small[0] + small[1] + small[2] + small[3]
    for k in range(3):
        o_gain[k] = total[GAIN + k:GAIN + k + 1]
        o_shift[k] = total[SHIFT + k:SHIFT + k + 1]
    for k in range(4):
        o_upb[:, 512 * k:512 * k + 512] = total[UPB + k:UPB + k + 1]
    o_downb[...] = total[DOWNB:DOWNB + 1]
    o_haltw[...] = total[HALTW:HALTW + 1]
    o_haltb[...] = total[SCAL:SCAL + 1, 0:1]
    ran, alive = total[SCAL:SCAL + 1, 1:2], total[SCAL:SCAL + 1, 2:3]
    o_act[...] = jnp.concatenate([ran / alive, 1.0 - alive / (32 * T)], axis=1)


def on_device(states, cotangent, halting, segments, norm_gain, norm_bias, attn_in, attn_out, cross, up_weight, up_bias,
              down_weight, down_bias, halt_weight, halt_bias):
    vm, anywhere = pl.BlockSpec(memory_space=pltpu.VMEM), pl.BlockSpec(memory_space=pl.ANY)
    arrived = pl.pallas_call(
        kernel,
        out_shape=[
            jax.ShapeDtypeStruct((2, 128, T), BF),
            jax.ShapeDtypeStruct((2, 128, T), BF),
            jax.ShapeDtypeStruct((2, 4, 32, 512), BF),
            jax.ShapeDtypeStruct((2, 32, 1024), BF),
            jax.ShapeDtypeStruct((2, 32, 256), BF),
            jax.ShapeDtypeStruct((4, SMALL, T), F32),
        ],
        in_specs=[anywhere] * 2 + [vm] * 8 + [anywhere] * 2 + [vm] + [anywhere] * 2,
        out_specs=[anywhere] * 6,
        scratch_shapes=[pltpu.VMEM(*spec) for spec in SCRATCH.values()]
        + [pltpu.SemaphoreType.DMA(shape) for shape in SEMS.values() for _ in (0, 1)],
        compiler_params=pltpu.CompilerParams(
            collective_id=0, has_side_effects=True, vmem_limit_bytes=62 * 2**20),
        name="step",
    )(states[0], cotangent[0], halting[0], segments, jnp.transpose(norm_gain, (1, 0, 2)),
      jnp.transpose(norm_bias, (1, 0, 2)), up_bias.reshape(4, 1, T), down_bias, halt_weight,
      halt_bias.reshape(1, 1), jnp.transpose(attn_in[0], (1, 0, 2)), attn_out[0].T, cross[0], up_weight[0],
      down_weight[0].T)
    st, dx, gain, shift, g_in, g_out, g_cross, g_up, upb, g_down, downb, haltw, haltb, act = pl.pallas_call(
        finish,
        out_shape=[
            jax.ShapeDtypeStruct((2, 128, T), BF),
            jax.ShapeDtypeStruct((2, 128, T), F32),
            jax.ShapeDtypeStruct((3, 1, T), F32),
            jax.ShapeDtypeStruct((3, 1, T), F32),
            jax.ShapeDtypeStruct((3, 32, 128), F32),
            jax.ShapeDtypeStruct((32, 128), F32),
            jax.ShapeDtypeStruct((32, 2, 128), F32),
            jax.ShapeDtypeStruct((32, 512), F32),
            jax.ShapeDtypeStruct((1, 2048), F32),
            jax.ShapeDtypeStruct((32, 512), F32),
            jax.ShapeDtypeStruct((1, T), F32),
            jax.ShapeDtypeStruct((1, T), F32),
            jax.ShapeDtypeStruct((1, 1), F32),
            jax.ShapeDtypeStruct((1, 2), F32),
        ],
        in_specs=[vm] * 6,
        out_specs=[vm] * 14,
        name="finish",
    )(*arrived)
    return (
        st[None], dx[None], jnp.transpose(gain, (1, 0, 2)), jnp.transpose(shift, (1, 0, 2)),
        jnp.transpose(g_in, (1, 0, 2))[None], g_out.T[None], g_cross[None], g_up[None], upb, g_down.T[None], downb,
        haltw, haltb.reshape(1), act,
    )


def solution(mesh):
    split = (
        P("pipe", "dp", "mp", None), P("pipe", "dp", "mp", None), P("pipe", "dp", "mp"), P(None, "dp", None),
        P("pipe", None, None), P("pipe", None, None), P("pipe", "dp", None, "mp"), P("pipe", "mp", "dp"),
        P("pipe", "dp", None, "mp"), P("pipe", "dp", "mp"), P("pipe", None), P("pipe", "mp", "dp"),
        P("pipe", None), P("pipe", None), P("pipe"),
    )
    out = (
        P("pipe", "dp", "mp", None), P("pipe", "dp", "mp", None), P("pipe", None, None), P("pipe", None, None),
        P("pipe", "dp", None, "mp"), P("pipe", "mp", "dp"), P("pipe", "dp", None, "mp"), P("pipe", "dp", "mp"),
        P("pipe", None), P("pipe", "mp", "dp"), P("pipe", None), P("pipe", None), P("pipe"), P("pipe", None),
    )
    return jax.shard_map(on_device, mesh=mesh, in_specs=split, out_specs=out, check_vma=False)
```

```python
import jax
import jax.numpy as jnp
from jax import lax
from jax.experimental import pallas as pl
from jax.experimental.pallas import tpu as pltpu
from jax.sharding import PartitionSpec as P

MESH = pl.DeviceIdType.MESH
BF = jnp.bfloat16
F32 = jnp.float32
EPS = 1e-06
T = 512
SCALE = 0.125
WIDTHS = (512, 1024, 512)

GAIN, SHIFT, UPB, DOWNB, HALTW, SCAL = 0, 3, 6, 10, 11, 12
SMALL = 16

SCRATCH = dict(
    PSB=((32, 512), BF),
    PFB=((32, 1024), BF),
    PCB=((32, 256), BF),
    PK=((SMALL, T), F32),
    HB=((2, 16, 128), BF),
    HL=((4, 16, 128), BF),
    RN=((T, 128), F32),
    IN=((T, T), BF),
    COT=((T, T), BF),
    PSIB=((SMALL, T), F32),
    PV=((SMALL, T), F32),
    W0=((2, 4, 4, 32, 512), BF),
    W1=((2, 4, 4, 32, 1024), BF),
    W2=((2, 4, 4, 32, 512), BF),
    U=((3, T, T), F32),
    F=((3, T, 128), F32),
    N=((3, T, T), BF),
    QKV=((2, T, 384), BF),
    KT=((2, 128, T), BF),
    VT=((2, 128, T), BF),
    HD=((2, T, 128), BF),
    PA=((2, 2, T, T), BF),
    CQ=((2, T, 128), BF),
    CKV=((2, T, 256), BF),
    CKT=((2, 128, T), BF),
    CVT=((2, 128, T), BF),
    HX=((2, T, 128), BF),
    PX=((2, 2, T, T), BF),
    AS=((T, T), F32),
    DIF=((T, T), F32),
    GP=((2, T, T), F32),
    ACT=((2, T, T), BF),
    PB=((2, T, T), BF),
    DA=((T, T), F32),
    DX=((T, T), F32),
    FF=((T, T), BF),
    FB=((T, T), BF),
    XS=((3, T, T), BF),
    XR=((3, T, T), BF),
    XO=((3, T, T), F32),
    DSF=((T, T), F32),
    BS=((T, T), F32),
    BX=((T, T), F32),
    MEM=((T, T), BF),
    DM=((T, T), BF),
    DS=((T, T), BF),
    DSR=((T, T), BF),
    DSO=((T, T), BF),
    DQ=((2, T, 384), BF),
    DH=((2, T, 128), BF),
    DSB=((2, 2, T, T), BF),
    PR=((T, 128), F32),
    OB=((T, T), BF),
    DXB=((T, T), BF),
    G0=((2, 4, 4, 32, 512), BF),
    G1=((2, 4, 4, 32, 1024), BF),
    G2=((2, 4, 4, 32, 512), BF),
    LA0=((2, 3, 4, 32, 512), BF),
    RX1=((2, 2, 2, 32, 1024), BF),
    RF1=((2, 2, 4, 32, 1024), BF),
    RX2=((2, 2, 2, 32, 512), BF),
    RF2=((2, 2, 4, 32, 512), BF),
    SA0=((2, 4, 32, 512), BF),
    SA1=((2, 4, 32, 1024), BF),
    SA2=((2, 4, 32, 512), BF),
    LB0=((2, 3, 32, 512), BF),
    LB1=((2, 3, 32, 1024), BF),
    LB2=((2, 3, 32, 512), BF),
    SB0=((2, 32, 512), BF),
    SB1=((2, 32, 1024), BF),
    SB2=((2, 32, 512), BF),
    SM=((SMALL, T), F32),
    LM1=((3, 8, T), F32),
    SM2=((8, T), F32),
    LM2=((3, 8, T), F32),
    SM3=((8, T), F32),
    SM4=((8, T), F32),
)

SEMS = dict(
    pp=(1,),
    g0=(2, 4),
    pf=(2,),
    pc=(2, 2),
    po=(2,),
    rk=(2, 2),
    st=(4,),
    hl=(4,),
    ct=(4,),
    lo=(6,),
    ga=(4, 3, 2, 3),
    ex=(3, 2),
    mem=(4, 2),
    mfw=(4,),
    dmx=(4,),
    dme=(4, 2),
    dmf=(4,),
    rs=(3, 2, 2, 6),
    rt=(3, 2, 3),
    ra=(3, 2, 3),
    rc=(3, 2),
    r0=(2, 4),
    os=(2,),
    od=(2,),
    m1=(3,),
    m2=(3,),
    m3=(4,),
)


def mm(a, b):
    return lax.dot_general(a, b, (((1,), (0,)), ((), ())), preferred_element_type=F32)


def mm_nt(a, b):
    return lax.dot_general(a, b, (((1,), (1,)), ((), ())), preferred_element_type=F32)


def mm_tn(a, b):
    return lax.dot_general(a, b, (((0,), (0,)), ((), ())), preferred_element_type=F32)


def rows_of(i, size):
    return pl.ds(pl.multiple_of(i * size, size), size)


def loop(count, body):
    lax.fori_loop(0, count, lambda i, _: (body(i), 0)[1], 0)


def wide(v):
    return jnp.concatenate([v, v, v, v], axis=1)


def mean(v):
    return jnp.mean(v, axis=-1, keepdims=True)


class Refs:
    pass


def kernel(*refs):
    (states, cot, halts, seg, gain, shift, upb, downb, haltw, haltb, w_in, w_out, w_cross, w_up, w_down,
     o_st, o_dx, o_c0, o_c1, o_c2, o_sm) = refs[:21]
    r = Refs()
    rest = refs[21:]
    for name, ref in zip(SCRATCH, rest):
        setattr(r, name, ref)
    rest = rest[len(SCRATCH):]
    ss, rs = {}, {}
    for k, name in enumerate(SEMS):
        ss[name], rs[name] = rest[2 * k], rest[2 * k + 1]
    W, G = (r.W0, r.W1, r.W2), (r.G0, r.G1, r.G2)
    RX, RF, SA = (None, r.RX1, r.RX2), (None, r.RF1, r.RF2), (r.SA0, r.SA1, r.SA2)
    LB, SB = (r.LB0, r.LB1, r.LB2), (r.SB0, r.SB1, r.SB2)
    LC = (o_c0, o_c1, o_c2)

    c = lax.axis_index("pipe")
    dp = lax.axis_index("dp")
    x = lax.axis_index("mp")
    y, z = dp // 4, lax.rem(dp, 4)
    dec = jnp.logical_or(x == 1, x == 2)
    enc = jnp.logical_not(dec)
    role = jnp.where(dec, 1, 0)
    m = x // 2
    sib = 1 - c
    pair = x + 1 - 2 * lax.rem(x, 2)
    zs = [lax.rem(z + d, 4) for d in range(4)]
    zb = [lax.rem(z + 4 - d, 4) for d in range(4)]
    ys = [lax.rem(y + d, 4) for d in range(4)]
    yb = [lax.rem(y + 4 - d, 4) for d in range(4)]

    def dev(core=c, yy=y, zz=z, xx=x):
        return (core, yy * 4 + zz, xx)

    def rdma(src, dst, ssem, rsem, to):
        return pltpu.make_async_remote_copy(
            src_ref=src, dst_ref=dst, send_sem=ssem, recv_sem=rsem, device_id=to, device_id_type=MESH
        )

    ends = []

    def put(what, when=None):
        rdma(*what()).start()

        def end():
            if when is None:
                rdma(*what()).wait_send()
            else:
                @pl.when(when)
                def _():
                    rdma(*what()).wait_send()

        ends.append(end)

    def put_or_keep(what, when=None):
        def away():
            core, xx = what()[4:]
            return jnp.logical_not(jnp.logical_and(core == c, xx == x))

        @pl.when(jnp.logical_not(away()))
        def _():
            src, dst, _, rsem, _, _ = what()
            pltpu.make_async_copy(src, dst, rsem).start()

        def remote():
            src, dst, ssem, rsem, core, xx = what()
            return rdma(src, dst, ssem, rsem, dev(core, xx=xx))

        @pl.when(away())
        def _():
            remote().start()

        def end():
            out = away()
            if when is not None:
                out = jnp.logical_and(out, when)

            @pl.when(out)
            def _():
                remote().wait_send()

        ends.append(end)

    def got(dst, rsem):
        pltpu.make_async_copy(dst, dst, rsem).wait()

    barrier = pltpu.get_barrier_semaphore()
    partners = [dev(zz=zs[d]) for d in (1, 2, 3)] + [dev(yy=ys[d]) for d in (1, 2, 3)]
    partners += [dev(core=sib, xx=lax.rem(x + d, 4)) for d in range(4)]
    partners += [dev(xx=lax.rem(x + d, 4)) for d in (1, 2, 3)]
    jj_me = lax.rem(x, 2)
    for to in partners:
        pl.semaphore_signal(barrier, inc=1, device_id=to, device_id_type=MESH)

    staged = [
        (w_in.at[0], r.PSB.at[:, pl.ds(0, 128)]), (w_in.at[1], r.PSB.at[:, pl.ds(128, 128)]),
        (w_in.at[2], r.PSB.at[:, pl.ds(256, 128)]), (w_out, r.PSB.at[:, pl.ds(384, 128)]),
        (w_up, r.PFB.at[:, pl.ds(0, 512)]), (w_down, r.PFB.at[:, pl.ds(512, 512)])]
    staged = [pltpu.make_async_copy(a, b, rs["lo"].at[k]) for k, (a, b) in enumerate(staged)]
    for copy in staged:
        copy.start()
    r.PK[GAIN:GAIN + 3] = gain[:, 0, :]
    r.PK[SHIFT:SHIFT + 3] = shift[:, 0, :]
    r.PK[UPB:UPB + 4] = upb[:, 0, :]
    r.PK[DOWNB:DOWNB + 1] = downb[...]
    r.PK[HALTW:HALTW + 1] = haltw[...]
    r.PK[SCAL:SCAL + 1] = jnp.broadcast_to(haltb[...], (1, T))
    r.PK[SCAL + 1:SMALL] = jnp.zeros((SMALL - SCAL - 1, T), F32)
    for k in (0, 1):
        r.HB[k] = jnp.broadcast_to(halts[k:k + 1].astype(F32), (16, 128)).astype(BF)
    crossed = w_cross[...].astype(F32)
    for k in (0, 1):
        r.PCB[:, 128 * k:128 * k + 128] = crossed[:, k, :].astype(BF)
    for copy in staged:
        copy.wait()
    pl.semaphore_wait(barrier, len(partners))

    homes = (c, 3 - c)

    def gathered(g):
        return r.W1.at[..., pl.ds(512 * (g // 2), 512)] if g in (1, 3) else W[g]

    def gather_first(g):
        for d in (1, 2, 3):
            for jj in (0, 1):
                def what(d=d, jj=jj):
                    mine = gathered(g).at[jj, y, z]
                    return (mine, mine, ss["ga"].at[g, 0, jj, d - 1], rs["ga"].at[g, 0, jj, d - 1],
                            dev(zz=zs[d]) if jj == 0 else dev(yy=ys[d]))

                put(what, dec if g == 2 else None)

    low_half, high_half = pl.ds(0, 2), pl.ds(2, 2)

    def block(ref, jj, at, half=None):
        if jj == 0:
            return ref.at[0, at] if half is None else ref.at[0, at, half]
        return ref.at[1, :, at] if half is None else ref.at[1, half, at]

    def along(jj, d):
        if jj == 0:
            return ys[d % 4], dev(yy=ys[d % 4])
        return zs[d % 4], dev(zz=zs[d % 4])

    def gather_second(g):
        for d in range(4):
            if d > 0:
                got(gathered(g).at[0, y, zb[d]], rs["ga"].at[g, 0, 0, d - 1])
                got(gathered(g).at[1, yb[d], z], rs["ga"].at[g, 0, 1, d - 1])
        for jj in (0, 1):
            for k, d in ((0, 1), (1, 3)):
                def what(jj=jj, k=k, d=d):
                    mine = block(gathered(g), jj, along(jj, 0)[0])
                    return mine, mine, ss["ga"].at[g, 1, jj, k], rs["ga"].at[g, 1, jj, k], along(jj, d)[1]

                put(what, dec if g == 2 else None)

    def gather_pass(g):
        for jj in (0, 1):
            for k, d in ((0, 1), (1, 3)):
                behind = along(jj, 4 - d)[0]
                got(block(gathered(g), jj, behind), rs["ga"].at[g, 1, jj, k])

                def what(jj=jj, k=k, d=d):
                    part = block(gathered(g), jj, along(jj, 4 - d)[0], (low_half, high_half)[k])
                    return part, part, ss["ga"].at[g, 2, jj, k], rs["ga"].at[g, 2, jj, k], along(jj, d)[1]

                put(what, dec if g == 2 else None)

    def gather_done(g):
        for jj in (0, 1):
            for k in (0, 1):
                got(block(gathered(g), jj, along(jj, 2)[0], (low_half, high_half)[k]), rs["ga"].at[g, 2, jj, k])

    def reduce_first(g, jj, h=0, when=None):
        cols = pl.ds(512 * h, 512)
        for k, d in ((0, 1), (1, 3)):
            halves = (low_half, high_half)

            def far(k=k, d=d):
                return (block(G[g].at[..., cols], jj, along(jj, 2)[0], halves[k]), RX[g].at[jj, k, :, :, cols],
                        ss["rs"].at[g, h, jj, k], rs["rs"].at[g, h, jj, k], along(jj, d)[1])

            put(far, when)
        for k, d in ((0, 1), (1, 3)):
            def near(k=k, d=d):
                return (block(G[g].at[..., cols], jj, along(jj, d)[0], halves[1 - k]),
                        RF[g].at[jj, k, halves[1 - k], :, cols],
                        ss["rs"].at[g, h, jj, 2 + k], rs["rs"].at[g, h, jj, 2 + k], along(jj, d)[1])

            put(near, when)

    def reduce_pass(g, h=0, when=None):
        cols = pl.ds(512 * h, 512)
        for jj in (0, 1):
            for k, d in ((0, 1), (1, 3)):
                got(RX[g].at[jj, k, :, :, cols], rs["rs"].at[g, h, jj, k])
                at = along(jj, d)[0]
                own = G[g][0, at, 2 * k:2 * k + 2, :, cols] if jj == 0 else G[g][1, 2 * k:2 * k + 2, at, :, cols]
                RX[g][jj, k, :, :, cols] = (own.astype(F32) + RX[g][jj, k, :, :, cols].astype(F32)).astype(BF)

                def what(jj=jj, k=k, d=d):
                    return (RX[g].at[jj, k, :, :, cols], RF[g].at[jj, k, (low_half, high_half)[k], :, cols],
                            ss["rs"].at[g, h, jj, 4 + k], rs["rs"].at[g, h, jj, 4 + k], along(jj, d)[1])

                put(what, when)

    direct_cols = (pl.ds(384, 128), pl.ds(128, 256), pl.ds(0, 128))

    def reduce_direct(e):
        cols = direct_cols[e]
        for jj in (0, 1):
            for d in (1, 2, 3):
                def what(jj=jj, d=d):
                    at, to = along(jj, d)
                    return (block(r.G0.at[..., cols], jj, at), r.LA0.at[jj, d - 1, :, :, cols],
                            ss["ra"].at[e, jj, d - 1], rs["ra"].at[e, jj, d - 1], to)

                put(what)

    def reduce_second(g):
        for jj in (0, 1):
            if g == 0:
                for d in range(3):
                    for e in range(3):
                        got(r.LA0.at[jj, d, :, :, direct_cols[e]], rs["ra"].at[e, jj, d])
            for k in (0, 1) if g > 0 else ():
                for h in (0, 1) if g == 1 else (0,):
                    cols = pl.ds(512 * h, 512)
                    halves = (low_half, high_half)
                    got(RF[g].at[jj, k, halves[1 - k], :, cols], rs["rs"].at[g, h, jj, 2 + k])
                    got(RF[g].at[jj, k, halves[k], :, cols], rs["rs"].at[g, h, jj, 4 + k])

            def add(i):
                own = G[g][0, y, i] if jj == 0 else G[g][1, i, z]
                total = own.astype(F32)
                for k in range(3 if g == 0 else 2):
                    total = total + (r.LA0 if g == 0 else RF[g])[jj, k, i].astype(F32)
                SA[g][jj, i] = total.astype(BF)

            loop(4, add)
            if True:
                for d in (1, 2, 3):
                    def what(d=d, jj=jj):
                        src, to = ((SA[g].at[0, zs[d]], dev(zz=zs[d])) if jj == 0 else
                                   (SA[g].at[1, ys[d]], dev(yy=ys[d])))
                        return (src, LB[g].at[jj, d - 1], ss["rt"].at[g, jj, d - 1],
                                rs["rt"].at[g, jj, d - 1], to)

                    put(what, dec if g == 2 else None)

    def reduce_third(g):
        for jj in (0, 1):
            for d in (1, 2, 3):
                got(LB[g].at[jj, d - 1], rs["rt"].at[g, jj, d - 1])
            total = (SA[g][0, z] if jj == 0 else SA[g][1, y]).astype(F32)
            for d in range(3):
                total = total + LB[g][jj, d].astype(F32)
            SB[g][jj] = total.astype(BF)
            if g == 2:
                for k in (0, 1):
                    put_or_keep(lambda jj=jj, k=k: (
                        SB[g].at[jj, :, pl.ds(256 * k, 256)], LC[g].at[m], ss["rk"].at[k, jj], rs["rc"].at[g, m],
                        k, 2 * c + jj), dec)
            else:
                put_or_keep(lambda jj=jj: (
                    SB[g].at[jj], LC[g].at[m], ss["rc"].at[g, jj], rs["rc"].at[g, m], role, 2 * c + jj))

    def half_rows(i, core):
        return pl.ds(pl.multiple_of(256 * (i // 2) + 128 * core + 64 * lax.rem(i, 2), 64), 64)

    def memory_copy(i):
        part = half_rows(i, c)
        return rdma(r.N.at[1, part], r.MEM.at[part], ss["mem"].at[i, 0], rs["mem"].at[i, c], dev(xx=pair))

    def memory_forward(i):
        part = half_rows(i, c)
        return rdma(r.MEM.at[part], r.MEM.at[part], ss["mfw"].at[i], rs["mem"].at[i, c], dev(core=sib))

    def memory_grad_swap(i):
        part = half_rows(i, sib)
        return rdma(r.DS.at[part], r.DSR.at[part], ss["dmx"].at[i], rs["dmx"].at[i], dev(core=sib))

    def memory_grad_copy(i):
        part = half_rows(i, c)
        return rdma(r.DSO.at[part], r.DM.at[part], ss["dme"].at[i, 0], rs["dme"].at[i, c], dev(xx=pair))

    def memory_grad_forward(i):
        part = half_rows(i, c)
        return rdma(r.DM.at[part], r.DM.at[part], ss["dmf"].at[i], rs["dme"].at[i, c], dev(core=sib))

    def exchange_copy(k, i):
        part = rows_of(i, 256)
        return rdma(r.XS.at[k, part], r.XR.at[k, part], ss["ex"].at[k, i], rs["ex"].at[k, i], dev(core=sib))

    for k in (0, 1):
        put_or_keep(lambda k=k: (
            r.PSB, r.W0.at[jj_me, y, z], ss["g0"].at[k, 0], rs["g0"].at[jj_me, 0], x // 2, homes[k]))
    for k in (0, 1):
        put_or_keep(lambda k=k: (
            r.PFB, r.W1.at[jj_me, y, z], ss["pf"].at[k], rs["pf"].at[jj_me], x // 2, homes[k]))
    put(lambda: (r.PK, r.PSIB, ss["pp"].at[0], rs["pp"].at[0], dev(core=sib)))
    r.SM[...] = jnp.zeros((SMALL, T), F32)
    for jj in (0, 1):
        got(r.W0.at[jj, y, z], rs["g0"].at[jj, 0])
    gather_first(0)
    for jj in (0, 1):
        got(r.W1.at[jj, y, z], rs["pf"].at[jj])
    gather_first(1)
    gather_first(3)
    for k in (0, 1):
        for core in (0, 1):
            put_or_keep(lambda k=k, core=core: (
                states.at[k], r.IN.at[rows_of(x, 128)], ss["st"].at[2 * k + core], rs["st"].at[x], core, homes[k]))
            put_or_keep(lambda k=k, core=core: (
                r.HB.at[k], r.HL.at[x], ss["hl"].at[2 * k + core], rs["hl"].at[x], core, homes[k]))
    gather_second(0)
    for k in (0, 1):
        put_or_keep(lambda k=k: (
            r.PCB, r.W2.at[jj_me, y, z, :, pl.ds(pl.multiple_of(256 * c, 256), 256)], ss["po"].at[k],
            rs["pc"].at[jj_me, c], x // 2, k + 1))
    gather_second(1)
    gather_pass(0)
    gather_second(3)
    for k in (0, 1):
        for core in (0, 1):
            put_or_keep(lambda k=k, core=core: (
                cot.at[k], r.COT.at[rows_of(x, 128)], ss["ct"].at[2 * k + core], rs["ct"].at[x], core, homes[k]))
    got(r.PSIB, rs["pp"].at[0])
    r.PV[...] = jnp.where(c == role, r.PK[...], r.PSIB[...])
    for q in range(4):
        got(r.IN.at[pl.ds(128 * q, 128)], rs["st"].at[q])
        got(r.HL.at[q], rs["hl"].at[q])

    def param(row):
        return r.PV[pl.ds(row, 1), :]

    def ln_to(li, part, size, v):
        center = v - mean(v)
        factor = lax.rsqrt(mean(center * center) + EPS)
        unit = center * factor
        normed = unit * param(GAIN + li) + param(SHIFT + li)
        r.U[li, part] = unit
        r.F[li, part] = jnp.broadcast_to(factor, (size, 128))
        r.N[li, part] = normed.astype(BF)

    def count(row, v):
        r.SM[pl.ds(row, 1), :] += jnp.sum(v, axis=0, keepdims=True)

    def ln_back(li, part, n):
        unit, factor = r.U[li, part], wide(r.F[li, part])
        scaled = n * param(GAIN + li)
        count(GAIN + li, n * unit)
        count(SHIFT + li, n)
        return factor * (scaled - mean(scaled) - unit * mean(scaled * unit))

    def weight(g, jj, lo, hi):
        return W[g][jj, :, :, :, lo:hi].reshape(T, hi - lo)

    def both(g, lo, hi):
        return jnp.concatenate([weight(g, 0, lo, hi), weight(g, 1, lo, hi)], axis=1)

    def send_part(k, i, value):
        r.XO[k, rows_of(i, 256)] = value
        r.XS[k, rows_of(i, 256)] = value.astype(BF)
        exchange_copy(k, i).start()

    def received(k, part):
        return r.XO[k, part] + r.XR[k, part].astype(F32)

    def after_exchange(k, i, body):
        exchange_copy(k, i).wait()
        body(rows_of(i, 256))

    low_lane = lax.broadcasted_iota(jnp.int32, (1, 128), 1) < 64

    def head_part(v, hh):
        return jnp.where(low_lane if hh == 0 else jnp.logical_not(low_lane), v, jnp.zeros_like(v))

    def attend(q_of, kv, k_at, vt, bias, probs, heads):
        for jj in (0, 1):
            q, keys = q_of(jj), kv[jj, :, k_at:k_at + 128]
            outs = []
            for hh in (0, 1):
                s = mm_nt(keys, head_part(q, hh)) + bias[...]
                e = jnp.exp(s - jnp.max(s, axis=0, keepdims=True))
                w = (e * (1.0 / jnp.sum(e, axis=0, keepdims=True))).astype(BF)
                probs[jj, hh] = w
                outs.append(mm(vt[jj, 64 * hh:64 * hh + 64, :], w))
            heads[jj] = jnp.concatenate(outs, axis=0).T.astype(BF)

    def attend_back(q_of, kv, v_at, probs, dk_at, dv_at):
        for jj in (0, 1):
            q, o, values = q_of(jj), r.DH[jj], kv[jj, :, v_at:v_at + 128]
            for hh in (0, 1):
                w = probs[jj, hh].astype(F32)
                wd = w * mm_nt(values, head_part(o, hh))
                delta = jnp.sum(wd, axis=0, keepdims=True)
                r.DSB[jj, hh] = (wd - w * delta).astype(BF)
            dks = [mm(r.DSB[jj, hh], q) for hh in (0, 1)]
            dvs = [mm(probs[jj, hh], o) for hh in (0, 1)]
            r.DQ[jj, :, dk_at:dk_at + 128] = jnp.where(low_lane, dks[0], dks[1]).astype(BF)
            r.DQ[jj, :, dv_at:dv_at + 128] = jnp.where(low_lane, dvs[0], dvs[1]).astype(BF)

    def queries_back(kt, dq_at):
        for jj in (0, 1):
            dqs = [mm(kt[jj, 64 * hh:64 * hh + 64, :], r.DSB[jj, hh]) for hh in (0, 1)]
            r.DQ[jj, :, dq_at:dq_at + 128] = (jnp.concatenate(dqs, axis=0).T * SCALE).astype(BF)

    def outer(g, jj, lo, hi, left, right):
        G[g][jj, :, :, :, lo:hi] = mm_tn(left[...], right()).astype(BF).reshape(4, 4, 32, hi - lo)

    def first(i):
        part = rows_of(i, 256)
        v = r.IN[part].astype(F32)
        ln_to(0, part, 256, v)
        logit = jnp.sum(v * param(HALTW), axis=-1, keepdims=True) + param(SCAL)[:, 0:1]
        r.PR[part] = jnp.broadcast_to(jax.nn.sigmoid(logit), (256, 128))
        for h in (0, 1):
            r.RN[rows_of(2 * i + h, 128)] = mm_tn(r.HL[2 * i + h], jnp.full((16, 128), 1.0 / 16.0, BF))

    loop(2, first)

    docs = lax.broadcasted_iota(jnp.int32, (16, T), 0)
    seg_src, seg_tgt = seg[0, pl.ds(m, 1), :], seg[1, pl.ds(m, 1), :]
    own_src = jnp.where(docs == seg_src, 1.0, 0.0).astype(BF)
    own_tgt = jnp.where(docs == seg_tgt, 1.0, 0.0).astype(BF)
    own_self = jnp.where(enc, own_src, own_tgt)
    k_at = lax.broadcasted_iota(jnp.int32, (T, T), 1)
    q_at = lax.broadcasted_iota(jnp.int32, (T, T), 0)
    reach = jnp.where(enc, T, 0)
    same = jnp.logical_and(mm_tn(own_self, own_self) > 0.5, q_at <= k_at + reach)
    r.BS[...] = jnp.where(same, 0.0, -1e30)

    @pl.when(dec)
    def _():
        r.BX[...] = jnp.where(mm_tn(own_src, own_tgt) > 0.5, 0.0, -1e30)

    @pl.when(dec)
    def _():
        for jj in (0, 1):
            for k in (0, 1):
                got(r.W2.at[jj, y, z, :, pl.ds(256 * k, 256)], rs["pc"].at[jj, k])
        gather_first(2)

    gather_pass(1)
    gather_done(0)

    for jj in (0, 1):
        three = mm(r.N[0], weight(0, jj, 0, 384))
        r.QKV[jj, :, 0:128] = (three[:, 0:128] * SCALE).astype(BF)
        r.QKV[jj, :, 128:384] = three[:, 128:384].astype(BF)
        r.KT[jj] = three[:, 128:256].T.astype(BF)
        r.VT[jj] = three[:, 256:384].T.astype(BF)

    attend(lambda jj: r.QKV[jj, :, 0:128], r.QKV, 128, r.VT, r.BS, r.PA, r.HD)

    gather_pass(3)

    @pl.when(dec)
    def _():
        gather_second(2)

    def self_out(i):
        part = rows_of(i, 256)
        heads = jnp.concatenate([r.HD[0, part], r.HD[1, part]], axis=1)
        send_part(0, i, mm_nt(heads, both(0, 384, 512)))

    loop(2, self_out)
    second = jnp.where(enc, 2, 1)

    def self_after(part):
        v = r.IN[part].astype(F32) + received(0, part)
        r.AS[part] = v
        ln_to(second, part, 256, v)

    @pl.when(dec)
    def _():
        gather_pass(2)
        gather_done(2)
        loop(2, lambda i: after_exchange(0, i, self_after))
        for jj in (0, 1):
            def ask(i):
                part = rows_of(i, 256)
                r.CQ[jj, part] = (mm(r.N[1, part], weight(2, jj, 256, 384)) * SCALE).astype(BF)

            loop(2, ask)

        def memory_in(i):
            for p in (0, 1):
                got(r.MEM.at[half_rows(2 * i + p, c)], rs["mem"].at[2 * i + p, c])
                memory_forward(2 * i + p).start()
            for p in (0, 1):
                got(r.MEM.at[half_rows(2 * i + p, sib)], rs["mem"].at[2 * i + p, sib])
            part = rows_of(i, 256)
            for jj in (0, 1):
                pairs = mm(r.MEM[part], weight(2, jj, 0, 256))
                r.CKV[jj, part] = pairs.astype(BF)
                r.CKT[jj, :, part] = pairs[:, 0:128].T.astype(BF)
                r.CVT[jj, :, part] = pairs[:, 128:256].T.astype(BF)

        loop(2, memory_in)
        attend(lambda jj: r.CQ[jj], r.CKV, 0, r.CVT, r.BX, r.PX, r.HX)

        def cross_out(i):
            part = rows_of(i, 256)
            heads = jnp.concatenate([r.HX[0, part], r.HX[1, part]], axis=1)
            send_part(2, i, mm_nt(heads, both(2, 384, 512)))

        loop(2, cross_out)

    gather_done(1)
    gather_done(3)

    def cross_after(part):
        v = r.AS[part] + received(2, part)
        r.AS[part] = v
        ln_to(2, part, 256, v)

    def ffn(i):
        pl.when(enc)(lambda: after_exchange(0, i, self_after))
        pl.when(dec)(lambda: after_exchange(2, i, cross_after))
        part = rows_of(i, 256)
        total = None
        for jj in (0, 1):
            bias = r.PV[pl.ds(UPB + 2 * c + jj, 1), :]
            u = mm(r.N[2, part], weight(1, jj, 0, 512)) + bias
            sq = u * u
            t = jnp.tanh(0.7978845608028654 * (u + 0.044715 * sq * u))
            r.GP[jj, part] = 0.5 * (1.0 + t) + 0.5 * u * (1.0 - t * t) * (
                0.7978845608028654 * (1.0 + 3 * 0.044715 * sq))
            act = (0.5 * u * (1.0 + t)).astype(BF)
            r.ACT[jj, part] = act
            term = mm_nt(act, weight(1, jj, 512, 1024))
            total = term if total is None else total + term
        send_part(1, i, total)

    loop(2, ffn)

    def running(part):
        mask = r.RN[part]
        return mask, mask * r.PR[part]

    def ffn_after(part):
        v = r.IN[part].astype(F32)
        diff = r.AS[part] + received(1, part) + param(DOWNB) - v
        r.DIF[part] = diff
        mask, run = running(part)
        lane = lax.broadcasted_iota(jnp.int32, (1, 128), 1)
        tally = jnp.where(lane == 1, run, jnp.where(lane == 2, mask, 0.0))
        r.SM[SCAL:SCAL + 1, 0:128] += jnp.sum(tally, axis=0, keepdims=True)
        return v + wide(run) * diff

    @pl.when(enc)
    def _():
        def memory_out(i):
            exchange_copy(1, i).wait()
            part = rows_of(i, 256)
            ln_to(1, part, 256, ffn_after(part))
            for p in (0, 1):
                memory_copy(2 * i + p).start()

        loop(2, memory_out)
        r.OB[...] = r.N[1]

    for q in range(4):
        got(r.COT.at[pl.ds(128 * q, 128)], rs["ct"].at[q])

    def halt_back(part, g):
        v = r.IN[part].astype(F32)
        mask, run = running(part)
        prob = r.PR[part]
        run = wide(run)
        d_aff = g * run
        r.DA[part] = d_aff
        r.FF[part] = d_aff.astype(BF)
        dot = jnp.sum(g * r.DIF[part], axis=-1, keepdims=True)
        zz = mask * dot * prob * (1.0 - prob)
        zw = wide(zz)
        r.DX[part] = g * (1.0 - run) + zw * param(HALTW)
        count(DOWNB, d_aff)
        count(HALTW, zw * v)
        lane = lax.broadcasted_iota(jnp.int32, (1, 128), 1)
        r.SM[SCAL:SCAL + 1, 0:128] += jnp.sum(jnp.where(lane == 0, zz, 0.0), axis=0, keepdims=True)

    def memory_grad_pass(i):
        for h in (0, 1):
            got(r.DM.at[half_rows(2 * i + h, c)], rs["dme"].at[2 * i + h, c])
            memory_grad_forward(2 * i + h).start()

    def memory_grad_in(i):
        for h in (0, 1):
            got(r.DM.at[half_rows(2 * i + h, sib)], rs["dme"].at[2 * i + h, sib])
        part = rows_of(i, 256)
        n = r.COT[part].astype(F32) + r.DM[part].astype(F32)
        halt_back(part, ln_back(1, part, n))

    def output_in(i):
        exchange_copy(1, i).wait()
        part = rows_of(i, 256)
        r.OB[part] = ffn_after(part).astype(BF)
        halt_back(part, r.COT[part].astype(F32))

    def down_weights():
        for jj in (0, 1):
            outer(1, jj, 512, 1024, r.FF, lambda: r.ACT[jj])

    def up_weights():
        for jj in (0, 1):
            outer(1, jj, 0, 512, r.N.at[2], lambda: r.PB[jj])

    pl.when(enc)(lambda: memory_grad_pass(0))

    def ffn_back(i):
        pl.when(enc)(lambda: memory_grad_in(i))
        pl.when(dec)(lambda: output_in(i))

        @pl.when(jnp.logical_and(enc, i == 1))
        def _():
            down_weights()
            for jj in (0, 1):
                reduce_first(1, jj, 1, enc)

        part = rows_of(i, 256)
        total = None
        for jj in (0, 1):
            dp_ = mm(r.FF[part], weight(1, jj, 512, 1024)) * r.GP[jj, part]
            row = UPB + 2 * c + jj
            r.SM[pl.ds(row, 1), :] += jnp.sum(dp_, axis=0, keepdims=True)
            low = dp_.astype(BF)
            r.PB[jj, part] = low
            term = mm_nt(low, weight(1, jj, 0, 512))
            total = term if total is None else total + term
        send_part(0, i, total)
        pl.when(jnp.logical_and(enc, i == 0))(lambda: memory_grad_pass(1))

    loop(2, ffn_back)
    for h in (0, 1):
        quarter = 2 * c + h
        put_or_keep(lambda h=h, quarter=quarter: (
            r.OB.at[rows_of(quarter, 128)], o_st.at[m], ss["os"].at[h], rs["os"].at[m], role, quarter))

    @pl.when(enc)
    def _():
        up_weights()
        for jj in (0, 1):
            reduce_first(1, jj, 0, enc)

    def ffn_back_after(part):
        d = r.DA[part] + ln_back(2, part, received(0, part))
        r.DA[part] = d
        r.FB[part] = d.astype(BF)

    def heads_back(g, i):
        part = rows_of(i, 256)
        both_heads = mm(r.FB[part], both(g, 384, 512)).astype(BF)
        r.DH[0, part], r.DH[1, part] = both_heads[:, 0:128], both_heads[:, 128:256]

    def after_ffn_back(i):
        after_exchange(0, i, ffn_back_after)
        pl.when(enc)(lambda: heads_back(0, i))
        pl.when(dec)(lambda: heads_back(2, i))

    loop(2, after_ffn_back)
    pl.when(enc)(lambda: reduce_pass(1, 1, enc))

    @pl.when(dec)
    def _():
        attend_back(lambda jj: r.CQ[jj], r.CKV, 128, r.PX, 0, 128)

        def memory_back(core):
            groups = [pl.ds(pl.multiple_of(256 * i + 128 * core, 128), 128) for i in (0, 1)]
            pairs = jnp.concatenate([
                jnp.concatenate([r.DQ[0, part, 0:256], r.DQ[1, part, 0:256]], axis=1) for part in groups], axis=0)
            grad = mm_nt(pairs, both(2, 0, 256))
            r.DSF[groups[0]], r.DSF[groups[1]] = grad[0:128], grad[128:256]
            grad = grad.astype(BF)
            r.DS[groups[0]], r.DS[groups[1]] = grad[0:128], grad[128:256]

        memory_back(sib)
        for p in range(4):
            memory_grad_swap(p).start()
        memory_back(c)

        def memory_grad_out(i):
            part = half_rows(i, c)
            got(r.DSR.at[part], rs["dmx"].at[i])
            r.DSO[part] = (r.DSF[part] + r.DSR[part].astype(F32)).astype(BF)
            memory_grad_copy(i).start()

        loop(4, memory_grad_out)
        queries_back(r.CKT, 256)
        down_weights()
        for jj in (0, 1):
            reduce_first(1, jj, 1, dec)
        up_weights()
        for jj in (0, 1):
            reduce_first(1, jj, 0, dec)

        def query_back(i):
            part = rows_of(i, 256)
            asked = jnp.concatenate([r.DQ[0, part, 256:384], r.DQ[1, part, 256:384]], axis=1)
            send_part(1, i, mm_nt(asked, both(2, 256, 384)))

        loop(2, query_back)
        for jj in (0, 1):
            outer(2, jj, 0, 256, r.MEM, lambda: r.DQ[jj, :, 0:256])
            outer(2, jj, 256, 384, r.N.at[1], lambda: r.DQ[jj, :, 256:384])
            outer(2, jj, 384, 512, r.FB, lambda: r.HX[jj])
            reduce_first(2, jj, 0, dec)

        def cross_back_after(part):
            d = r.DA[part] + ln_back(1, part, received(1, part))
            r.DA[part] = d
            r.FB[part] = d.astype(BF)

        reduce_pass(1, 1, dec)

        def after_query_back(i):
            after_exchange(1, i, cross_back_after)
            heads_back(0, i)

        loop(2, after_query_back)

    for jj in (0, 1):
        outer(0, jj, 384, 512, r.FB, lambda: r.HD[jj])
    reduce_direct(0)
    attend_back(lambda jj: r.QKV[jj, :, 0:128], r.QKV, 256, r.PA, 128, 256)

    for jj in (0, 1):
        outer(0, jj, 128, 384, r.N.at[0], lambda: r.DQ[jj, :, 128:384])
    reduce_pass(1, 0)
    reduce_direct(1)
    queries_back(r.KT, 0)
    for jj in (0, 1):
        outer(0, jj, 0, 128, r.N.at[0], lambda: r.DQ[jj, :, 0:128])
    reduce_direct(2)

    def first_back(i):
        part = rows_of(i, 256)
        all_three = jnp.concatenate([r.DQ[0, part], r.DQ[1, part]], axis=1)
        send_part(2, i, mm_nt(all_three, both(0, 0, 384)))

    loop(2, first_back)

    @pl.when(dec)
    def _():
        reduce_pass(2, 0, dec)

    def first_back_after(part):
        d = r.DX[part] + r.DA[part] + ln_back(0, part, received(2, part))
        r.DXB[part] = d.astype(BF)

    loop(2, lambda i: after_exchange(2, i, first_back_after))
    for h in (0, 1):
        quarter = 2 * c + h
        put_or_keep(lambda h=h, quarter=quarter: (r.DXB.at[rows_of(quarter, 128)], o_dx.at[m], ss["od"].at[h], rs["od"].at[m], role, quarter))

    for row in range(6):
        late = r.SM[DOWNB + row:DOWNB + row + 1] if row < 3 else jnp.zeros((1, T), F32)
        r.SM2[row:row + 1] = jnp.where(c == 0, r.SM[row:row + 1], late)
    for row in (0, 1):
        r.SM2[6 + row:7 + row] = r.SM[pl.ds(UPB + 2 * c + row, 1), :]
    for d in (1, 2, 3):
        put(lambda d=d: (r.SM2, r.LM1.at[d - 1], ss["m1"].at[d - 1], rs["m1"].at[d - 1], dev(zz=zs[d])))
    reduce_second(1)
    for d in range(3):
        got(r.LM1.at[d], rs["m1"].at[d])
    r.SM3[...] = r.SM2[...] + r.LM1[0] + r.LM1[1] + r.LM1[2]
    for d in (1, 2, 3):
        put(lambda d=d: (r.SM3, r.LM2.at[d - 1], ss["m2"].at[d - 1], rs["m2"].at[d - 1], dev(yy=ys[d])))

    @pl.when(dec)
    def _():
        reduce_second(2)

    reduce_second(0)
    for d in range(3):
        got(r.LM2.at[d], rs["m2"].at[d])
    r.SM4[...] = r.SM3[...] + r.LM2[0] + r.LM2[1] + r.LM2[2]
    for k in range(4):
        put_or_keep(lambda k=k: (r.SM4, o_sm.at[2 * m + c], ss["m3"].at[k], rs["m3"].at[2 * m + c], role, k))
    reduce_third(1)

    @pl.when(dec)
    def _():
        reduce_third(2)

    reduce_third(0)

    @pl.when(enc)
    def _():
        for i in range(4):
            memory_copy(i).wait_send()
            memory_grad_forward(i).wait_send()

    @pl.when(dec)
    def _():
        for i in range(4):
            memory_forward(i).wait_send()
            memory_grad_swap(i).wait_send()
            memory_grad_copy(i).wait_send()

    for end in ends:
        end()
    for k in (0, 1):
        got(o_st.at[k], rs["os"].at[k])
        got(o_dx.at[k], rs["od"].at[k])
    for k in range(4):
        got(o_sm.at[k], rs["m3"].at[k])
    for k in (0, 1):
        for g in range(3):
            got(LC[g].at[k], rs["rc"].at[g, k])


def finish(st, dx, c0, c1, c2, small, o_st, o_dx, o_gain, o_shift, o_in, o_out, o_cross, o_up, o_upb, o_down, o_downb,
           o_haltw, o_haltb, o_act):
    o_st[...] = st[...]
    o_dx[...] = dx[...].astype(F32)
    both = c0[0].astype(F32) + c0[1].astype(F32)
    for k in range(3):
        o_in[k] = both[:, 128 * k:128 * k + 128]
    o_out[...] = both[:, 384:512]
    both = c1[0].astype(F32) + c1[1].astype(F32)
    o_up[...], o_down[...] = both[:, 0:512], both[:, 512:1024]
    both = c2[0].astype(F32) + c2[1].astype(F32)
    for k in (0, 1):
        o_cross[:, k, :] = both[:, 128 * k:128 * k + 128]
    norms, rest = small[0] + small[2], small[1] + small[3]
    for k in range(3):
        o_gain[k] = norms[GAIN + k:GAIN + k + 1]
        o_shift[k] = norms[SHIFT + k:SHIFT + k + 1]
    for k in (0, 1):
        o_upb[:, 512 * k:512 * k + 512] = norms[6 + k:7 + k]
        o_upb[:, 1024 + 512 * k:1536 + 512 * k] = rest[6 + k:7 + k]
    o_downb[...] = rest[0:1]
    o_haltw[...] = rest[1:2]
    o_haltb[...] = rest[2:3, 0:1]
    ran, alive = rest[2:3, 1:2], rest[2:3, 2:3]
    o_act[...] = jnp.concatenate([ran / alive, 1.0 - alive / (32 * T)], axis=1)


def on_device(states, cotangent, halting, segments, norm_gain, norm_bias, attn_in, attn_out, cross, up_weight, up_bias,
              down_weight, down_bias, halt_weight, halt_bias):
    vm, anywhere = pl.BlockSpec(memory_space=pltpu.VMEM), pl.BlockSpec(memory_space=pl.ANY)
    arrived = pl.pallas_call(
        kernel,
        out_shape=[
            jax.ShapeDtypeStruct((2, 128, T), BF),
            jax.ShapeDtypeStruct((2, 128, T), BF),
            jax.ShapeDtypeStruct((2, 32, 512), BF),
            jax.ShapeDtypeStruct((2, 32, 1024), BF),
            jax.ShapeDtypeStruct((2, 32, 256), BF),
            jax.ShapeDtypeStruct((4, 8, T), F32),
        ],
        in_specs=[anywhere] * 2 + [vm] * 8 + [anywhere] * 2 + [vm] + [anywhere] * 2,
        out_specs=[anywhere] * 6,
        scratch_shapes=[pltpu.VMEM(*spec) for spec in SCRATCH.values()]
        + [pltpu.SemaphoreType.DMA(shape) for shape in SEMS.values() for _ in (0, 1)],
        compiler_params=pltpu.CompilerParams(
            collective_id=0, has_side_effects=True, vmem_limit_bytes=62 * 2**20),
        name="step",
    )(states[0], cotangent[0], halting[0], segments, jnp.transpose(norm_gain, (1, 0, 2)),
      jnp.transpose(norm_bias, (1, 0, 2)), up_bias.reshape(4, 1, T), down_bias, halt_weight,
      halt_bias.reshape(1, 1), jnp.transpose(attn_in[0], (1, 0, 2)), attn_out[0].T, cross[0], up_weight[0],
      down_weight[0].T)
    st, dx, gain, shift, g_in, g_out, g_cross, g_up, upb, g_down, downb, haltw, haltb, act = pl.pallas_call(
        finish,
        out_shape=[
            jax.ShapeDtypeStruct((2, 128, T), BF),
            jax.ShapeDtypeStruct((2, 128, T), F32),
            jax.ShapeDtypeStruct((3, 1, T), F32),
            jax.ShapeDtypeStruct((3, 1, T), F32),
            jax.ShapeDtypeStruct((3, 32, 128), F32),
            jax.ShapeDtypeStruct((32, 128), F32),
            jax.ShapeDtypeStruct((32, 2, 128), F32),
            jax.ShapeDtypeStruct((32, 512), F32),
            jax.ShapeDtypeStruct((1, 2048), F32),
            jax.ShapeDtypeStruct((32, 512), F32),
            jax.ShapeDtypeStruct((1, T), F32),
            jax.ShapeDtypeStruct((1, T), F32),
            jax.ShapeDtypeStruct((1, 1), F32),
            jax.ShapeDtypeStruct((1, 2), F32),
        ],
        in_specs=[vm] * 6,
        out_specs=[vm] * 14,
        name="finish",
    )(*arrived)
    return (
        st[None], dx[None], jnp.transpose(gain, (1, 0, 2)), jnp.transpose(shift, (1, 0, 2)),
        jnp.transpose(g_in, (1, 0, 2))[None], g_out.T[None], g_cross[None], g_up[None], upb, g_down.T[None], downb,
        haltw, haltb.reshape(1), act,
    )


def solution(mesh):
    split = (
        P("pipe", "dp", "mp", None), P("pipe", "dp", "mp", None), P("pipe", "dp", "mp"), P(None, "dp", None),
        P("pipe", None, None), P("pipe", None, None), P("pipe", "dp", None, "mp"), P("pipe", "mp", "dp"),
        P("pipe", "dp", None, "mp"), P("pipe", "dp", "mp"), P("pipe", None), P("pipe", "mp", "dp"),
        P("pipe", None), P("pipe", None), P("pipe"),
    )
    out = (
        P("pipe", "dp", "mp", None), P("pipe", "dp", "mp", None), P("pipe", None, None), P("pipe", None, None),
        P("pipe", "dp", None, "mp"), P("pipe", "mp", "dp"), P("pipe", "dp", None, "mp"), P("pipe", "dp", "mp"),
        P("pipe", None), P("pipe", "mp", "dp"), P("pipe", None), P("pipe", None), P("pipe"), P("pipe", None),
    )
    return jax.shard_map(on_device, mesh=mesh, in_specs=split, out_specs=out, check_vma=False)
```

```python
import jax
import jax.numpy as jnp
from jax import lax
from jax.experimental import pallas as pl
from jax.experimental.pallas import tpu as pltpu
from jax.sharding import PartitionSpec as P

MESH = pl.DeviceIdType.MESH
BF = jnp.bfloat16
F32 = jnp.float32
EPS = 1e-06
T = 512
SCALE = 0.125
WIDTHS = (512, 1024, 512)

GAIN, SHIFT, UPB, DOWNB, HALTW, SCAL = 0, 3, 6, 10, 11, 12
SMALL = 16

SCRATCH = dict(
    PSB=((32, 512), BF),
    PFB=((32, 1024), BF),
    PCB=((32, 256), BF),
    PK=((SMALL, T), F32),
    HB=((2, 16, 128), BF),
    HL=((4, 16, 128), BF),
    RN=((T, 128), F32),
    IN=((T, T), BF),
    COT=((T, T), BF),
    PSIB=((SMALL, T), F32),
    PV=((SMALL, T), F32),
    W0=((2, 4, 4, 32, 512), BF),
    W1=((2, 4, 4, 32, 1024), BF),
    W2=((2, 4, 4, 32, 512), BF),
    U=((3, T, T), F32),
    F=((3, T, 128), F32),
    N=((3, T, T), BF),
    QKV=((2, T, 384), BF),
    KT=((2, 128, T), BF),
    VT=((2, 128, T), BF),
    HD=((2, T, 128), BF),
    PA=((2, 2, T, T), BF),
    CQ=((2, T, 128), BF),
    CKV=((2, T, 256), BF),
    CKT=((2, 128, T), BF),
    CVT=((2, 128, T), BF),
    HX=((2, T, 128), BF),
    PX=((2, 2, T, T), BF),
    AS=((T, T), F32),
    DIF=((T, T), F32),
    GP=((2, T, T), F32),
    ACT=((2, T, T), BF),
    PB=((2, T, T), BF),
    DA=((T, T), F32),
    DX=((T, T), F32),
    FF=((T, T), BF),
    FB=((T, T), BF),
    XS=((3, T, T), BF),
    XR=((3, T, T), BF),
    XO=((3, T, T), F32),
    DSF=((T, T), F32),
    BS=((T, T), F32),
    BX=((T, T), F32),
    MEM=((T, T), BF),
    DM=((T, T), BF),
    DS=((T, T), BF),
    DSR=((T, T), BF),
    DSO=((T, T), BF),
    DQ=((2, T, 384), BF),
    DH=((2, T, 128), BF),
    DSB=((2, 2, T, T), BF),
    PR=((T, 128), F32),
    OB=((T, T), BF),
    DXB=((T, T), BF),
    G0=((2, 4, 4, 32, 512), BF),
    G1=((2, 4, 4, 32, 1024), BF),
    G2=((2, 4, 4, 32, 512), BF),
    LA0=((2, 3, 4, 32, 512), BF),
    RX1=((2, 2, 2, 32, 1024), BF),
    RF1=((2, 2, 4, 32, 1024), BF),
    RX2=((2, 2, 2, 32, 512), BF),
    RF2=((2, 2, 4, 32, 512), BF),
    SA0=((2, 4, 32, 512), BF),
    SA1=((2, 4, 32, 1024), BF),
    SA2=((2, 4, 32, 512), BF),
    LB0=((2, 3, 32, 512), BF),
    LB1=((2, 3, 32, 1024), BF),
    LB2=((2, 3, 32, 512), BF),
    SB0=((2, 32, 512), BF),
    SB1=((2, 32, 1024), BF),
    SB2=((2, 32, 512), BF),
    SM=((SMALL, T), F32),
    LM1=((3, 8, T), F32),
    SM2=((8, T), F32),
    LM2=((3, 8, T), F32),
    SM3=((8, T), F32),
    SM4=((8, T), F32),
)

SEMS = dict(
    pp=(1,),
    g0=(2, 4),
    pf=(2,),
    pc=(2, 2),
    po=(2,),
    rk=(2, 2),
    st=(4,),
    hl=(4,),
    ct=(4,),
    lo=(6,),
    ga=(4, 3, 2, 3),
    ex=(3, 2),
    mem=(4, 2),
    mfw=(4,),
    dmx=(4,),
    dme=(4, 2),
    dmf=(4,),
    rs=(3, 2, 2, 6),
    rt=(3, 2, 3),
    ra=(3, 2, 3),
    rc=(3, 2),
    r0=(2, 4),
    os=(2,),
    od=(2,),
    m1=(3,),
    m2=(3,),
    m3=(4,),
)


def mm(a, b):
    return lax.dot_general(a, b, (((1,), (0,)), ((), ())), preferred_element_type=F32)


def mm_nt(a, b):
    return lax.dot_general(a, b, (((1,), (1,)), ((), ())), preferred_element_type=F32)


def mm_tn(a, b):
    return lax.dot_general(a, b, (((0,), (0,)), ((), ())), preferred_element_type=F32)


def rows_of(i, size):
    return pl.ds(pl.multiple_of(i * size, size), size)


def loop(count, body):
    lax.fori_loop(0, count, lambda i, _: (body(i), 0)[1], 0)


def wide(v):
    return jnp.concatenate([v, v, v, v], axis=1)


def mean(v):
    return jnp.mean(v, axis=-1, keepdims=True)


class Refs:
    pass


def kernel(*refs):
    (states, cot, halts, seg, gain, shift, upb, downb, haltw, haltb, w_in, w_out, w_cross, w_up, w_down,
     o_st, o_dx, o_c0, o_c1, o_c2, o_sm) = refs[:21]
    r = Refs()
    rest = refs[21:]
    for name, ref in zip(SCRATCH, rest):
        setattr(r, name, ref)
    rest = rest[len(SCRATCH):]
    ss, rs = {}, {}
    for k, name in enumerate(SEMS):
        ss[name], rs[name] = rest[2 * k], rest[2 * k + 1]
    W, G = (r.W0, r.W1, r.W2), (r.G0, r.G1, r.G2)
    RX, RF, SA = (None, r.RX1, r.RX2), (None, r.RF1, r.RF2), (r.SA0, r.SA1, r.SA2)
    LB, SB = (r.LB0, r.LB1, r.LB2), (r.SB0, r.SB1, r.SB2)
    LC = (o_c0, o_c1, o_c2)

    c = lax.axis_index("pipe")
    dp = lax.axis_index("dp")
    x = lax.axis_index("mp")
    y, z = dp // 4, lax.rem(dp, 4)
    dec = jnp.logical_or(x == 1, x == 2)
    enc = jnp.logical_not(dec)
    role = jnp.where(dec, 1, 0)
    m = x // 2
    sib = 1 - c
    pair = x + 1 - 2 * lax.rem(x, 2)
    zs = [lax.rem(z + d, 4) for d in range(4)]
    zb = [lax.rem(z + 4 - d, 4) for d in range(4)]
    ys = [lax.rem(y + d, 4) for d in range(4)]
    yb = [lax.rem(y + 4 - d, 4) for d in range(4)]

    def dev(core=c, yy=y, zz=z, xx=x):
        return (core, yy * 4 + zz, xx)

    def rdma(src, dst, ssem, rsem, to):
        return pltpu.make_async_remote_copy(
            src_ref=src, dst_ref=dst, send_sem=ssem, recv_sem=rsem, device_id=to, device_id_type=MESH
        )

    ends = []

    def put(what, when=None):
        rdma(*what()).start()

        def end():
            if when is None:
                rdma(*what()).wait_send()
            else:
                @pl.when(when)
                def _():
                    rdma(*what()).wait_send()

        ends.append(end)

    def put_or_keep(what, when=None):
        def away():
            core, xx = what()[4:]
            return jnp.logical_not(jnp.logical_and(core == c, xx == x))

        @pl.when(jnp.logical_not(away()))
        def _():
            src, dst, _, rsem, _, _ = what()
            pltpu.make_async_copy(src, dst, rsem).start()

        def remote():
            src, dst, ssem, rsem, core, xx = what()
            return rdma(src, dst, ssem, rsem, dev(core, xx=xx))

        @pl.when(away())
        def _():
            remote().start()

        def end():
            out = away()
            if when is not None:
                out = jnp.logical_and(out, when)

            @pl.when(out)
            def _():
                remote().wait_send()

        ends.append(end)

    def got(dst, rsem):
        pltpu.make_async_copy(dst, dst, rsem).wait()

    barrier = pltpu.get_barrier_semaphore()
    partners = [dev(zz=zs[d]) for d in (1, 2, 3)] + [dev(yy=ys[d]) for d in (1, 2, 3)]
    partners += [dev(core=sib, xx=lax.rem(x + d, 4)) for d in range(4)]
    partners += [dev(xx=lax.rem(x + d, 4)) for d in (1, 2, 3)]
    jj_me = lax.rem(x, 2)
    for to in partners:
        pl.semaphore_signal(barrier, inc=1, device_id=to, device_id_type=MESH)

    staged = [
        (w_in.at[0], r.PSB.at[:, pl.ds(0, 128)]), (w_in.at[1], r.PSB.at[:, pl.ds(128, 128)]),
        (w_in.at[2], r.PSB.at[:, pl.ds(256, 128)]), (w_out, r.PSB.at[:, pl.ds(384, 128)]),
        (w_up, r.PFB.at[:, pl.ds(0, 512)]), (w_down, r.PFB.at[:, pl.ds(512, 512)])]
    staged = [pltpu.make_async_copy(a, b, rs["lo"].at[k]) for k, (a, b) in enumerate(staged)]
    for copy in staged:
        copy.start()
    r.PK[GAIN:GAIN + 3] = gain[:, 0, :]
    r.PK[SHIFT:SHIFT + 3] = shift[:, 0, :]
    r.PK[UPB:UPB + 4] = upb[:, 0, :]
    r.PK[DOWNB:DOWNB + 1] = downb[...]
    r.PK[HALTW:HALTW + 1] = haltw[...]
    r.PK[SCAL:SCAL + 1] = jnp.broadcast_to(haltb[...], (1, T))
    r.PK[SCAL + 1:SMALL] = jnp.zeros((SMALL - SCAL - 1, T), F32)
    for k in (0, 1):
        r.HB[k] = jnp.broadcast_to(halts[k:k + 1].astype(F32), (16, 128)).astype(BF)
    crossed = w_cross[...].astype(F32)
    for k in (0, 1):
        r.PCB[:, 128 * k:128 * k + 128] = crossed[:, k, :].astype(BF)
    for copy in staged:
        copy.wait()
    pl.semaphore_wait(barrier, len(partners))

    homes = (c, 3 - c)

    def gathered(g):
        return r.W1.at[..., pl.ds(512 * (g // 2), 512)] if g in (1, 3) else W[g]

    def gather_first(g):
        for d in (1, 2, 3):
            for jj in (0, 1):
                def what(d=d, jj=jj):
                    mine = gathered(g).at[jj, y, z]
                    return (mine, mine, ss["ga"].at[g, 0, jj, d - 1], rs["ga"].at[g, 0, jj, d - 1],
                            dev(zz=zs[d]) if jj == 0 else dev(yy=ys[d]))

                put(what, dec if g == 2 else None)

    low_half, high_half = pl.ds(0, 2), pl.ds(2, 2)

    def block(ref, jj, at, half=None):
        if jj == 0:
            return ref.at[0, at] if half is None else ref.at[0, at, half]
        return ref.at[1, :, at] if half is None else ref.at[1, half, at]

    def along(jj, d):
        if jj == 0:
            return ys[d % 4], dev(yy=ys[d % 4])
        return zs[d % 4], dev(zz=zs[d % 4])

    def gather_second(g):
        for d in range(4):
            if d > 0:
                got(gathered(g).at[0, y, zb[d]], rs["ga"].at[g, 0, 0, d - 1])
                got(gathered(g).at[1, yb[d], z], rs["ga"].at[g, 0, 1, d - 1])
        for jj in (0, 1):
            for k, d in ((0, 1), (1, 3)):
                def what(jj=jj, k=k, d=d):
                    mine = block(gathered(g), jj, along(jj, 0)[0])
                    return mine, mine, ss["ga"].at[g, 1, jj, k], rs["ga"].at[g, 1, jj, k], along(jj, d)[1]

                put(what, dec if g == 2 else None)

    def gather_pass(g):
        for jj in (0, 1):
            for k, d in ((0, 1), (1, 3)):
                behind = along(jj, 4 - d)[0]
                got(block(gathered(g), jj, behind), rs["ga"].at[g, 1, jj, k])

                def what(jj=jj, k=k, d=d):
                    part = block(gathered(g), jj, along(jj, 4 - d)[0], (low_half, high_half)[k])
                    return part, part, ss["ga"].at[g, 2, jj, k], rs["ga"].at[g, 2, jj, k], along(jj, d)[1]

                put(what, dec if g == 2 else None)

    def gather_done(g):
        for jj in (0, 1):
            for k in (0, 1):
                got(block(gathered(g), jj, along(jj, 2)[0], (low_half, high_half)[k]), rs["ga"].at[g, 2, jj, k])

    def reduce_first(g, jj, h=0, when=None):
        cols = pl.ds(512 * h, 512)
        for k, d in ((0, 1), (1, 3)):
            halves = (low_half, high_half)

            def far(k=k, d=d):
                return (block(G[g].at[..., cols], jj, along(jj, 2)[0], halves[k]), RX[g].at[jj, k, :, :, cols],
                        ss["rs"].at[g, h, jj, k], rs["rs"].at[g, h, jj, k], along(jj, d)[1])

            put(far, when)
        for k, d in ((0, 1), (1, 3)):
            def near(k=k, d=d):
                return (block(G[g].at[..., cols], jj, along(jj, d)[0], halves[1 - k]),
                        RF[g].at[jj, k, halves[1 - k], :, cols],
                        ss["rs"].at[g, h, jj, 2 + k], rs["rs"].at[g, h, jj, 2 + k], along(jj, d)[1])

            put(near, when)

    def reduce_pass(g, h=0, when=None):
        cols = pl.ds(512 * h, 512)
        for jj in (0, 1):
            for k, d in ((0, 1), (1, 3)):
                got(RX[g].at[jj, k, :, :, cols], rs["rs"].at[g, h, jj, k])
                at = along(jj, d)[0]
                own = G[g][0, at, 2 * k:2 * k + 2, :, cols] if jj == 0 else G[g][1, 2 * k:2 * k + 2, at, :, cols]
                RX[g][jj, k, :, :, cols] = (own.astype(F32) + RX[g][jj, k, :, :, cols].astype(F32)).astype(BF)

                def what(jj=jj, k=k, d=d):
                    return (RX[g].at[jj, k, :, :, cols], RF[g].at[jj, k, (low_half, high_half)[k], :, cols],
                            ss["rs"].at[g, h, jj, 4 + k], rs["rs"].at[g, h, jj, 4 + k], along(jj, d)[1])

                put(what, when)

    direct_cols = (pl.ds(384, 128), pl.ds(128, 256), pl.ds(0, 128))

    def reduce_direct(e):
        cols = direct_cols[e]
        for jj in (0, 1):
            for d in (1, 2, 3):
                def what(jj=jj, d=d):
                    at, to = along(jj, d)
                    return (block(r.G0.at[..., cols], jj, at), r.LA0.at[jj, d - 1, :, :, cols],
                            ss["ra"].at[e, jj, d - 1], rs["ra"].at[e, jj, d - 1], to)

                put(what)

    def reduce_second(g):
        for jj in (0, 1):
            if g == 0:
                for d in range(3):
                    for e in range(3):
                        got(r.LA0.at[jj, d, :, :, direct_cols[e]], rs["ra"].at[e, jj, d])
            for k in (0, 1) if g > 0 else ():
                for h in (0, 1) if g == 1 else (0,):
                    cols = pl.ds(512 * h, 512)
                    halves = (low_half, high_half)
                    got(RF[g].at[jj, k, halves[1 - k], :, cols], rs["rs"].at[g, h, jj, 2 + k])
                    got(RF[g].at[jj, k, halves[k], :, cols], rs["rs"].at[g, h, jj, 4 + k])

            def add(i):
                own = G[g][0, y, i] if jj == 0 else G[g][1, i, z]
                total = own.astype(F32)
                for k in range(3 if g == 0 else 2):
                    total = total + (r.LA0 if g == 0 else RF[g])[jj, k, i].astype(F32)
                SA[g][jj, i] = total.astype(BF)

            loop(4, add)
            if True:
                for d in (1, 2, 3):
                    def what(d=d, jj=jj):
                        src, to = ((SA[g].at[0, zs[d]], dev(zz=zs[d])) if jj == 0 else
                                   (SA[g].at[1, ys[d]], dev(yy=ys[d])))
                        return (src, LB[g].at[jj, d - 1], ss["rt"].at[g, jj, d - 1],
                                rs["rt"].at[g, jj, d - 1], to)

                    put(what, dec if g == 2 else None)

    def reduce_third(g):
        for jj in (0, 1):
            for d in (1, 2, 3):
                got(LB[g].at[jj, d - 1], rs["rt"].at[g, jj, d - 1])
            total = (SA[g][0, z] if jj == 0 else SA[g][1, y]).astype(F32)
            for d in range(3):
                total = total + LB[g][jj, d].astype(F32)
            SB[g][jj] = total.astype(BF)
            if g == 2:
                for k in (0, 1):
                    put_or_keep(lambda jj=jj, k=k: (
                        SB[g].at[jj, :, pl.ds(256 * k, 256)], LC[g].at[m], ss["rk"].at[k, jj], rs["rc"].at[g, m],
                        k, 2 * c + jj), dec)
            else:
                put_or_keep(lambda jj=jj: (
                    SB[g].at[jj], LC[g].at[m], ss["rc"].at[g, jj], rs["rc"].at[g, m], role, 2 * c + jj))

    def half_rows(i, core):
        return pl.ds(pl.multiple_of(256 * (i // 2) + 128 * core + 64 * lax.rem(i, 2), 64), 64)

    def memory_copy(i):
        part = half_rows(i, c)
        return rdma(r.N.at[1, part], r.MEM.at[part], ss["mem"].at[i, 0], rs["mem"].at[i, c], dev(xx=pair))

    def memory_forward(i):
        part = half_rows(i, c)
        return rdma(r.MEM.at[part], r.MEM.at[part], ss["mfw"].at[i], rs["mem"].at[i, c], dev(core=sib))

    def memory_grad_swap(i):
        part = half_rows(i, sib)
        return rdma(r.DS.at[part], r.DSR.at[part], ss["dmx"].at[i], rs["dmx"].at[i], dev(core=sib))

    def memory_grad_copy(i):
        part = half_rows(i, c)
        return rdma(r.DSO.at[part], r.DM.at[part], ss["dme"].at[i, 0], rs["dme"].at[i, c], dev(xx=pair))

    def memory_grad_forward(i):
        part = half_rows(i, c)
        return rdma(r.DM.at[part], r.DM.at[part], ss["dmf"].at[i], rs["dme"].at[i, c], dev(core=sib))

    def exchange_copy(k, i):
        part = rows_of(i, 256)
        return rdma(r.XS.at[k, part], r.XR.at[k, part], ss["ex"].at[k, i], rs["ex"].at[k, i], dev(core=sib))

    for k in (0, 1):
        put_or_keep(lambda k=k: (
            r.PSB, r.W0.at[jj_me, y, z], ss["g0"].at[k, 0], rs["g0"].at[jj_me, 0], x // 2, homes[k]))
    for k in (0, 1):
        put_or_keep(lambda k=k: (
            r.PFB, r.W1.at[jj_me, y, z], ss["pf"].at[k], rs["pf"].at[jj_me], x // 2, homes[k]))
    put(lambda: (r.PK, r.PSIB, ss["pp"].at[0], rs["pp"].at[0], dev(core=sib)))
    r.SM[...] = jnp.zeros((SMALL, T), F32)
    for jj in (0, 1):
        got(r.W0.at[jj, y, z], rs["g0"].at[jj, 0])
    gather_first(0)
    for jj in (0, 1):
        got(r.W1.at[jj, y, z], rs["pf"].at[jj])
    gather_first(1)
    gather_first(3)
    for k in (0, 1):
        for core in (0, 1):
            put_or_keep(lambda k=k, core=core: (
                states.at[k], r.IN.at[rows_of(x, 128)], ss["st"].at[2 * k + core], rs["st"].at[x], core, homes[k]))
            put_or_keep(lambda k=k, core=core: (
                r.HB.at[k], r.HL.at[x], ss["hl"].at[2 * k + core], rs["hl"].at[x], core, homes[k]))
    gather_second(0)
    for k in (0, 1):
        put_or_keep(lambda k=k: (
            r.PCB, r.W2.at[jj_me, y, z, :, pl.ds(pl.multiple_of(256 * c, 256), 256)], ss["po"].at[k],
            rs["pc"].at[jj_me, c], x // 2, k + 1))
    gather_second(1)
    gather_pass(0)
    gather_second(3)
    for k in (0, 1):
        for core in (0, 1):
            put_or_keep(lambda k=k, core=core: (
                cot.at[k], r.COT.at[rows_of(x, 128)], ss["ct"].at[2 * k + core], rs["ct"].at[x], core, homes[k]))
    got(r.PSIB, rs["pp"].at[0])
    r.PV[...] = jnp.where(c == role, r.PK[...], r.PSIB[...])
    for q in range(4):
        got(r.IN.at[pl.ds(128 * q, 128)], rs["st"].at[q])
        got(r.HL.at[q], rs["hl"].at[q])

    def param(row):
        return r.PV[pl.ds(row, 1), :]

    def ln_to(li, part, size, v):
        center = v - mean(v)
        factor = lax.rsqrt(mean(center * center) + EPS)
        unit = center * factor
        normed = unit * param(GAIN + li) + param(SHIFT + li)
        r.U[li, part] = unit
        r.F[li, part] = jnp.broadcast_to(factor, (size, 128))
        r.N[li, part] = normed.astype(BF)

    def count(row, v):
        r.SM[pl.ds(row, 1), :] += jnp.sum(v, axis=0, keepdims=True)

    def ln_back(li, part, n):
        unit, factor = r.U[li, part], wide(r.F[li, part])
        scaled = n * param(GAIN + li)
        count(GAIN + li, n * unit)
        count(SHIFT + li, n)
        return factor * (scaled - mean(scaled) - unit * mean(scaled * unit))

    def weight(g, jj, lo, hi):
        return W[g][jj, :, :, :, lo:hi].reshape(T, hi - lo)

    def both(g, lo, hi):
        return jnp.concatenate([weight(g, 0, lo, hi), weight(g, 1, lo, hi)], axis=1)

    def send_part(k, i, value):
        r.XO[k, rows_of(i, 256)] = value
        r.XS[k, rows_of(i, 256)] = value.astype(BF)
        exchange_copy(k, i).start()

    def received(k, part):
        return r.XO[k, part] + r.XR[k, part].astype(F32)

    def after_exchange(k, i, body):
        exchange_copy(k, i).wait()
        body(rows_of(i, 256))

    low_lane = lax.broadcasted_iota(jnp.int32, (1, 128), 1) < 64

    def head_part(v, hh):
        return jnp.where(low_lane if hh == 0 else jnp.logical_not(low_lane), v, jnp.zeros_like(v))

    def attend(q_of, kv, k_at, vt, bias, probs, heads):
        for jj in (0, 1):
            q, keys = q_of(jj), kv[jj, :, k_at:k_at + 128]
            outs = []
            for hh in (0, 1):
                s = mm_nt(keys, head_part(q, hh)) + bias[...]
                e = jnp.exp(s - jnp.max(s, axis=0, keepdims=True))
                w = (e * (1.0 / jnp.sum(e, axis=0, keepdims=True))).astype(BF)
                probs[jj, hh] = w
                outs.append(mm(vt[jj, 64 * hh:64 * hh + 64, :], w))
            heads[jj] = jnp.concatenate(outs, axis=0).T.astype(BF)

    def attend_back(q_of, kv, v_at, probs, dk_at, dv_at):
        for jj in (0, 1):
            q, o, values = q_of(jj), r.DH[jj], kv[jj, :, v_at:v_at + 128]
            for hh in (0, 1):
                w = probs[jj, hh].astype(F32)
                wd = w * mm_nt(values, head_part(o, hh))
                delta = jnp.sum(wd, axis=0, keepdims=True)
                r.DSB[jj, hh] = (wd - w * delta).astype(BF)
            dks = [mm(r.DSB[jj, hh], q) for hh in (0, 1)]
            dvs = [mm(probs[jj, hh], o) for hh in (0, 1)]
            r.DQ[jj, :, dk_at:dk_at + 128] = jnp.where(low_lane, dks[0], dks[1]).astype(BF)
            r.DQ[jj, :, dv_at:dv_at + 128] = jnp.where(low_lane, dvs[0], dvs[1]).astype(BF)

    def queries_back(kt, dq_at):
        for jj in (0, 1):
            dqs = [mm(kt[jj, 64 * hh:64 * hh + 64, :], r.DSB[jj, hh]) for hh in (0, 1)]
            r.DQ[jj, :, dq_at:dq_at + 128] = (jnp.concatenate(dqs, axis=0).T * SCALE).astype(BF)

    def outer(g, jj, lo, hi, left, right):
        G[g][jj, :, :, :, lo:hi] = mm_tn(left[...], right()).astype(BF).reshape(4, 4, 32, hi - lo)

    def first(i):
        part = rows_of(i, 256)
        v = r.IN[part].astype(F32)
        ln_to(0, part, 256, v)
        logit = jnp.sum(v * param(HALTW), axis=-1, keepdims=True) + param(SCAL)[:, 0:1]
        r.PR[part] = jnp.broadcast_to(jax.nn.sigmoid(logit), (256, 128))
        for h in (0, 1):
            r.RN[rows_of(2 * i + h, 128)] = mm_tn(r.HL[2 * i + h], jnp.full((16, 128), 1.0 / 16.0, BF))

    loop(2, first)

    docs = lax.broadcasted_iota(jnp.int32, (16, T), 0)
    seg_src, seg_tgt = seg[0, pl.ds(m, 1), :], seg[1, pl.ds(m, 1), :]
    own_src = jnp.where(docs == seg_src, 1.0, 0.0).astype(BF)
    own_tgt = jnp.where(docs == seg_tgt, 1.0, 0.0).astype(BF)
    own_self = jnp.where(enc, own_src, own_tgt)
    k_at = lax.broadcasted_iota(jnp.int32, (T, T), 1)
    q_at = lax.broadcasted_iota(jnp.int32, (T, T), 0)
    reach = jnp.where(enc, T, 0)
    same = jnp.logical_and(mm_tn(own_self, own_self) > 0.5, q_at <= k_at + reach)
    r.BS[...] = jnp.where(same, 0.0, -1e30)

    @pl.when(dec)
    def _():
        r.BX[...] = jnp.where(mm_tn(own_src, own_tgt) > 0.5, 0.0, -1e30)

    @pl.when(dec)
    def _():
        for jj in (0, 1):
            for k in (0, 1):
                got(r.W2.at[jj, y, z, :, pl.ds(256 * k, 256)], rs["pc"].at[jj, k])
        gather_first(2)

    gather_pass(1)
    gather_done(0)

    for jj in (0, 1):
        three = mm(r.N[0], weight(0, jj, 0, 384))
        r.QKV[jj, :, 0:128] = (three[:, 0:128] * SCALE).astype(BF)
        r.QKV[jj, :, 128:384] = three[:, 128:384].astype(BF)
        r.KT[jj] = three[:, 128:256].T.astype(BF)
        r.VT[jj] = three[:, 256:384].T.astype(BF)

    gather_pass(3)
    attend(lambda jj: r.QKV[jj, :, 0:128], r.QKV, 128, r.VT, r.BS, r.PA, r.HD)

    @pl.when(dec)
    def _():
        gather_second(2)

    def self_out(i):
        part = rows_of(i, 256)
        heads = jnp.concatenate([r.HD[0, part], r.HD[1, part]], axis=1)
        send_part(0, i, mm_nt(heads, both(0, 384, 512)))

    loop(2, self_out)
    second = jnp.where(enc, 2, 1)

    def self_after(part):
        v = r.IN[part].astype(F32) + received(0, part)
        r.AS[part] = v
        ln_to(second, part, 256, v)

    @pl.when(dec)
    def _():
        gather_pass(2)
        gather_done(2)
        loop(2, lambda i: after_exchange(0, i, self_after))
        for jj in (0, 1):
            def ask(i):
                part = rows_of(i, 256)
                r.CQ[jj, part] = (mm(r.N[1, part], weight(2, jj, 256, 384)) * SCALE).astype(BF)

            loop(2, ask)

        def memory_in(i):
            for p in (0, 1):
                got(r.MEM.at[half_rows(2 * i + p, c)], rs["mem"].at[2 * i + p, c])
                memory_forward(2 * i + p).start()
            for p in (0, 1):
                got(r.MEM.at[half_rows(2 * i + p, sib)], rs["mem"].at[2 * i + p, sib])
            part = rows_of(i, 256)
            for jj in (0, 1):
                pairs = mm(r.MEM[part], weight(2, jj, 0, 256))
                r.CKV[jj, part] = pairs.astype(BF)
                r.CKT[jj, :, part] = pairs[:, 0:128].T.astype(BF)
                r.CVT[jj, :, part] = pairs[:, 128:256].T.astype(BF)

        loop(2, memory_in)
        attend(lambda jj: r.CQ[jj], r.CKV, 0, r.CVT, r.BX, r.PX, r.HX)

        def cross_out(i):
            part = rows_of(i, 256)
            heads = jnp.concatenate([r.HX[0, part], r.HX[1, part]], axis=1)
            send_part(2, i, mm_nt(heads, both(2, 384, 512)))

        loop(2, cross_out)

    gather_done(1)
    gather_done(3)

    def cross_after(part):
        v = r.AS[part] + received(2, part)
        r.AS[part] = v
        ln_to(2, part, 256, v)

    def ffn(i):
        pl.when(enc)(lambda: after_exchange(0, i, self_after))
        pl.when(dec)(lambda: after_exchange(2, i, cross_after))
        part = rows_of(i, 256)
        total = None
        for jj in (0, 1):
            bias = r.PV[pl.ds(UPB + 2 * c + jj, 1), :]
            u = mm(r.N[2, part], weight(1, jj, 0, 512)) + bias
            sq = u * u
            t = jnp.tanh(0.7978845608028654 * (u + 0.044715 * sq * u))
            r.GP[jj, part] = 0.5 * (1.0 + t) + 0.5 * u * (1.0 - t * t) * (
                0.7978845608028654 * (1.0 + 3 * 0.044715 * sq))
            act = (0.5 * u * (1.0 + t)).astype(BF)
            r.ACT[jj, part] = act
            term = mm_nt(act, weight(1, jj, 512, 1024))
            total = term if total is None else total + term
        send_part(1, i, total)

    loop(2, ffn)

    def running(part):
        mask = r.RN[part]
        return mask, mask * r.PR[part]

    def ffn_after(part):
        v = r.IN[part].astype(F32)
        diff = r.AS[part] + received(1, part) + param(DOWNB) - v
        r.DIF[part] = diff
        mask, run = running(part)
        lane = lax.broadcasted_iota(jnp.int32, (1, 128), 1)
        tally = jnp.where(lane == 1, run, jnp.where(lane == 2, mask, 0.0))
        r.SM[SCAL:SCAL + 1, 0:128] += jnp.sum(tally, axis=0, keepdims=True)
        return v + wide(run) * diff

    @pl.when(enc)
    def _():
        def memory_out(i):
            exchange_copy(1, i).wait()
            part = rows_of(i, 256)
            ln_to(1, part, 256, ffn_after(part))
            for p in (0, 1):
                memory_copy(2 * i + p).start()

        loop(2, memory_out)
        r.OB[...] = r.N[1]

    for q in range(4):
        got(r.COT.at[pl.ds(128 * q, 128)], rs["ct"].at[q])

    def halt_back(part, g):
        v = r.IN[part].astype(F32)
        mask, run = running(part)
        prob = r.PR[part]
        run = wide(run)
        d_aff = g * run
        r.DA[part] = d_aff
        r.FF[part] = d_aff.astype(BF)
        dot = jnp.sum(g * r.DIF[part], axis=-1, keepdims=True)
        zz = mask * dot * prob * (1.0 - prob)
        zw = wide(zz)
        r.DX[part] = g * (1.0 - run) + zw * param(HALTW)
        count(DOWNB, d_aff)
        count(HALTW, zw * v)
        lane = lax.broadcasted_iota(jnp.int32, (1, 128), 1)
        r.SM[SCAL:SCAL + 1, 0:128] += jnp.sum(jnp.where(lane == 0, zz, 0.0), axis=0, keepdims=True)

    def memory_grad_pass(i):
        for h in (0, 1):
            got(r.DM.at[half_rows(2 * i + h, c)], rs["dme"].at[2 * i + h, c])
            memory_grad_forward(2 * i + h).start()

    def memory_grad_in(i):
        for h in (0, 1):
            got(r.DM.at[half_rows(2 * i + h, sib)], rs["dme"].at[2 * i + h, sib])
        part = rows_of(i, 256)
        n = r.COT[part].astype(F32) + r.DM[part].astype(F32)
        halt_back(part, ln_back(1, part, n))

    def output_in(i):
        exchange_copy(1, i).wait()
        part = rows_of(i, 256)
        r.OB[part] = ffn_after(part).astype(BF)
        halt_back(part, r.COT[part].astype(F32))

    def down_weights():
        for jj in (0, 1):
            outer(1, jj, 512, 1024, r.FF, lambda: r.ACT[jj])

    def up_weights():
        for jj in (0, 1):
            outer(1, jj, 0, 512, r.N.at[2], lambda: r.PB[jj])

    pl.when(enc)(lambda: memory_grad_pass(0))

    def ffn_back(i):
        pl.when(enc)(lambda: memory_grad_in(i))
        pl.when(dec)(lambda: output_in(i))

        @pl.when(jnp.logical_and(enc, i == 1))
        def _():
            down_weights()
            for jj in (0, 1):
                reduce_first(1, jj, 1, enc)

        part = rows_of(i, 256)
        total = None
        for jj in (0, 1):
            dp_ = mm(r.FF[part], weight(1, jj, 512, 1024)) * r.GP[jj, part]
            row = UPB + 2 * c + jj
            r.SM[pl.ds(row, 1), :] += jnp.sum(dp_, axis=0, keepdims=True)
            low = dp_.astype(BF)
            r.PB[jj, part] = low
            term = mm_nt(low, weight(1, jj, 0, 512))
            total = term if total is None else total + term
        send_part(0, i, total)
        pl.when(jnp.logical_and(enc, i == 0))(lambda: memory_grad_pass(1))

    loop(2, ffn_back)
    for h in (0, 1):
        quarter = 2 * c + h
        put_or_keep(lambda h=h, quarter=quarter: (
            r.OB.at[rows_of(quarter, 128)], o_st.at[m], ss["os"].at[h], rs["os"].at[m], role, quarter))

    @pl.when(enc)
    def _():
        up_weights()
        for jj in (0, 1):
            reduce_first(1, jj, 0, enc)

    def ffn_back_after(part):
        d = r.DA[part] + ln_back(2, part, received(0, part))
        r.DA[part] = d
        r.FB[part] = d.astype(BF)

    def heads_back(g, i):
        part = rows_of(i, 256)
        both_heads = mm(r.FB[part], both(g, 384, 512)).astype(BF)
        r.DH[0, part], r.DH[1, part] = both_heads[:, 0:128], both_heads[:, 128:256]

    def after_ffn_back(i):
        after_exchange(0, i, ffn_back_after)
        pl.when(enc)(lambda: heads_back(0, i))
        pl.when(dec)(lambda: heads_back(2, i))

    loop(2, after_ffn_back)
    pl.when(enc)(lambda: reduce_pass(1, 1, enc))

    @pl.when(dec)
    def _():
        attend_back(lambda jj: r.CQ[jj], r.CKV, 128, r.PX, 0, 128)

        def memory_back(core):
            groups = [pl.ds(pl.multiple_of(256 * i + 128 * core, 128), 128) for i in (0, 1)]
            pairs = jnp.concatenate([
                jnp.concatenate([r.DQ[0, part, 0:256], r.DQ[1, part, 0:256]], axis=1) for part in groups], axis=0)
            grad = mm_nt(pairs, both(2, 0, 256))
            r.DSF[groups[0]], r.DSF[groups[1]] = grad[0:128], grad[128:256]
            grad = grad.astype(BF)
            r.DS[groups[0]], r.DS[groups[1]] = grad[0:128], grad[128:256]

        memory_back(sib)
        for p in range(4):
            memory_grad_swap(p).start()
        memory_back(c)

        def memory_grad_out(i):
            part = half_rows(i, c)
            got(r.DSR.at[part], rs["dmx"].at[i])
            r.DSO[part] = (r.DSF[part] + r.DSR[part].astype(F32)).astype(BF)
            memory_grad_copy(i).start()

        loop(4, memory_grad_out)
        queries_back(r.CKT, 256)
        down_weights()
        for jj in (0, 1):
            reduce_first(1, jj, 1, dec)
        up_weights()
        for jj in (0, 1):
            reduce_first(1, jj, 0, dec)

        def query_back(i):
            part = rows_of(i, 256)
            asked = jnp.concatenate([r.DQ[0, part, 256:384], r.DQ[1, part, 256:384]], axis=1)
            send_part(1, i, mm_nt(asked, both(2, 256, 384)))

        loop(2, query_back)
        for jj in (0, 1):
            outer(2, jj, 0, 256, r.MEM, lambda: r.DQ[jj, :, 0:256])
            outer(2, jj, 256, 384, r.N.at[1], lambda: r.DQ[jj, :, 256:384])
            outer(2, jj, 384, 512, r.FB, lambda: r.HX[jj])
            reduce_first(2, jj, 0, dec)

        def cross_back_after(part):
            d = r.DA[part] + ln_back(1, part, received(1, part))
            r.DA[part] = d
            r.FB[part] = d.astype(BF)

        reduce_pass(1, 1, dec)

        def after_query_back(i):
            after_exchange(1, i, cross_back_after)
            heads_back(0, i)

        loop(2, after_query_back)

    for jj in (0, 1):
        outer(0, jj, 384, 512, r.FB, lambda: r.HD[jj])
    reduce_direct(0)
    attend_back(lambda jj: r.QKV[jj, :, 0:128], r.QKV, 256, r.PA, 128, 256)

    for jj in (0, 1):
        outer(0, jj, 128, 384, r.N.at[0], lambda: r.DQ[jj, :, 128:384])
    reduce_pass(1, 0)
    reduce_direct(1)
    queries_back(r.KT, 0)
    for jj in (0, 1):
        outer(0, jj, 0, 128, r.N.at[0], lambda: r.DQ[jj, :, 0:128])
    reduce_direct(2)

    def first_back(i):
        part = rows_of(i, 256)
        all_three = jnp.concatenate([r.DQ[0, part], r.DQ[1, part]], axis=1)
        send_part(2, i, mm_nt(all_three, both(0, 0, 384)))

    loop(2, first_back)

    @pl.when(dec)
    def _():
        reduce_pass(2, 0, dec)

    def first_back_after(part):
        d = r.DX[part] + r.DA[part] + ln_back(0, part, received(2, part))
        r.DXB[part] = d.astype(BF)

    loop(2, lambda i: after_exchange(2, i, first_back_after))
    for h in (0, 1):
        quarter = 2 * c + h
        put_or_keep(lambda h=h, quarter=quarter: (r.DXB.at[rows_of(quarter, 128)], o_dx.at[m], ss["od"].at[h], rs["od"].at[m], role, quarter))

    for row in range(6):
        late = r.SM[DOWNB + row:DOWNB + row + 1] if row < 3 else jnp.zeros((1, T), F32)
        r.SM2[row:row + 1] = jnp.where(c == 0, r.SM[row:row + 1], late)
    for row in (0, 1):
        r.SM2[6 + row:7 + row] = r.SM[pl.ds(UPB + 2 * c + row, 1), :]
    for d in (1, 2, 3):
        put(lambda d=d: (r.SM2, r.LM1.at[d - 1], ss["m1"].at[d - 1], rs["m1"].at[d - 1], dev(zz=zs[d])))
    reduce_second(1)
    for d in range(3):
        got(r.LM1.at[d], rs["m1"].at[d])
    r.SM3[...] = r.SM2[...] + r.LM1[0] + r.LM1[1] + r.LM1[2]
    for d in (1, 2, 3):
        put(lambda d=d: (r.SM3, r.LM2.at[d - 1], ss["m2"].at[d - 1], rs["m2"].at[d - 1], dev(yy=ys[d])))

    @pl.when(dec)
    def _():
        reduce_second(2)

    reduce_second(0)
    for d in range(3):
        got(r.LM2.at[d], rs["m2"].at[d])
    r.SM4[...] = r.SM3[...] + r.LM2[0] + r.LM2[1] + r.LM2[2]
    for k in range(4):
        put_or_keep(lambda k=k: (r.SM4, o_sm.at[2 * m + c], ss["m3"].at[k], rs["m3"].at[2 * m + c], role, k))
    reduce_third(1)

    @pl.when(dec)
    def _():
        reduce_third(2)

    reduce_third(0)

    @pl.when(enc)
    def _():
        for i in range(4):
            memory_copy(i).wait_send()
            memory_grad_forward(i).wait_send()

    @pl.when(dec)
    def _():
        for i in range(4):
            memory_forward(i).wait_send()
            memory_grad_swap(i).wait_send()
            memory_grad_copy(i).wait_send()

    for end in ends:
        end()
    for k in (0, 1):
        got(o_st.at[k], rs["os"].at[k])
        got(o_dx.at[k], rs["od"].at[k])
    for k in range(4):
        got(o_sm.at[k], rs["m3"].at[k])
    for k in (0, 1):
        for g in range(3):
            got(LC[g].at[k], rs["rc"].at[g, k])


def finish(st, dx, c0, c1, c2, small, o_st, o_dx, o_gain, o_shift, o_in, o_out, o_cross, o_up, o_upb, o_down, o_downb,
           o_haltw, o_haltb, o_act):
    o_st[...] = st[...]
    o_dx[...] = dx[...].astype(F32)
    both = c0[0].astype(F32) + c0[1].astype(F32)
    for k in range(3):
        o_in[k] = both[:, 128 * k:128 * k + 128]
    o_out[...] = both[:, 384:512]
    both = c1[0].astype(F32) + c1[1].astype(F32)
    o_up[...], o_down[...] = both[:, 0:512], both[:, 512:1024]
    both = c2[0].astype(F32) + c2[1].astype(F32)
    for k in (0, 1):
        o_cross[:, k, :] = both[:, 128 * k:128 * k + 128]
    norms, rest = small[0] + small[2], small[1] + small[3]
    for k in range(3):
        o_gain[k] = norms[GAIN + k:GAIN + k + 1]
        o_shift[k] = norms[SHIFT + k:SHIFT + k + 1]
    for k in (0, 1):
        o_upb[:, 512 * k:512 * k + 512] = norms[6 + k:7 + k]
        o_upb[:, 1024 + 512 * k:1536 + 512 * k] = rest[6 + k:7 + k]
    o_downb[...] = rest[0:1]
    o_haltw[...] = rest[1:2]
    o_haltb[...] = rest[2:3, 0:1]
    ran, alive = rest[2:3, 1:2], rest[2:3, 2:3]
    o_act[...] = jnp.concatenate([ran / alive, 1.0 - alive / (32 * T)], axis=1)


def on_device(states, cotangent, halting, segments, norm_gain, norm_bias, attn_in, attn_out, cross, up_weight, up_bias,
              down_weight, down_bias, halt_weight, halt_bias):
    vm, anywhere = pl.BlockSpec(memory_space=pltpu.VMEM), pl.BlockSpec(memory_space=pl.ANY)
    arrived = pl.pallas_call(
        kernel,
        out_shape=[
            jax.ShapeDtypeStruct((2, 128, T), BF),
            jax.ShapeDtypeStruct((2, 128, T), BF),
            jax.ShapeDtypeStruct((2, 32, 512), BF),
            jax.ShapeDtypeStruct((2, 32, 1024), BF),
            jax.ShapeDtypeStruct((2, 32, 256), BF),
            jax.ShapeDtypeStruct((4, 8, T), F32),
        ],
        in_specs=[anywhere] * 2 + [vm] * 8 + [anywhere] * 2 + [vm] + [anywhere] * 2,
        out_specs=[anywhere] * 6,
        scratch_shapes=[pltpu.VMEM(*spec) for spec in SCRATCH.values()]
        + [pltpu.SemaphoreType.DMA(shape) for shape in SEMS.values() for _ in (0, 1)],
        compiler_params=pltpu.CompilerParams(
            collective_id=0, has_side_effects=True, vmem_limit_bytes=62 * 2**20),
        name="step",
    )(states[0], cotangent[0], halting[0], segments, jnp.transpose(norm_gain, (1, 0, 2)),
      jnp.transpose(norm_bias, (1, 0, 2)), up_bias.reshape(4, 1, T), down_bias, halt_weight,
      halt_bias.reshape(1, 1), jnp.transpose(attn_in[0], (1, 0, 2)), attn_out[0].T, cross[0], up_weight[0],
      down_weight[0].T)
    st, dx, gain, shift, g_in, g_out, g_cross, g_up, upb, g_down, downb, haltw, haltb, act = pl.pallas_call(
        finish,
        out_shape=[
            jax.ShapeDtypeStruct((2, 128, T), BF),
            jax.ShapeDtypeStruct((2, 128, T), F32),
            jax.ShapeDtypeStruct((3, 1, T), F32),
            jax.ShapeDtypeStruct((3, 1, T), F32),
            jax.ShapeDtypeStruct((3, 32, 128), F32),
            jax.ShapeDtypeStruct((32, 128), F32),
            jax.ShapeDtypeStruct((32, 2, 128), F32),
            jax.ShapeDtypeStruct((32, 512), F32),
            jax.ShapeDtypeStruct((1, 2048), F32),
            jax.ShapeDtypeStruct((32, 512), F32),
            jax.ShapeDtypeStruct((1, T), F32),
            jax.ShapeDtypeStruct((1, T), F32),
            jax.ShapeDtypeStruct((1, 1), F32),
            jax.ShapeDtypeStruct((1, 2), F32),
        ],
        in_specs=[vm] * 6,
        out_specs=[vm] * 14,
        name="finish",
    )(*arrived)
    return (
        st[None], dx[None], jnp.transpose(gain, (1, 0, 2)), jnp.transpose(shift, (1, 0, 2)),
        jnp.transpose(g_in, (1, 0, 2))[None], g_out.T[None], g_cross[None], g_up[None], upb, g_down.T[None], downb,
        haltw, haltb.reshape(1), act,
    )


def solution(mesh):
    split = (
        P("pipe", "dp", "mp", None), P("pipe", "dp", "mp", None), P("pipe", "dp", "mp"), P(None, "dp", None),
        P("pipe", None, None), P("pipe", None, None), P("pipe", "dp", None, "mp"), P("pipe", "mp", "dp"),
        P("pipe", "dp", None, "mp"), P("pipe", "dp", "mp"), P("pipe", None), P("pipe", "mp", "dp"),
        P("pipe", None), P("pipe", None), P("pipe"),
    )
    out = (
        P("pipe", "dp", "mp", None), P("pipe", "dp", "mp", None), P("pipe", None, None), P("pipe", None, None),
        P("pipe", "dp", None, "mp"), P("pipe", "mp", "dp"), P("pipe", "dp", None, "mp"), P("pipe", "dp", "mp"),
        P("pipe", None), P("pipe", "mp", "dp"), P("pipe", None), P("pipe", None), P("pipe"), P("pipe", None),
    )
    return jax.shard_map(on_device, mesh=mesh, in_specs=split, out_specs=out, check_vma=False)
```
